128 devices in a mesh: sky: 16 (over y, x), tm: 8 (over z, core).
Axes of the slice: x: 4, y: 4, z: 4, core: 2. Of those that a mesh axis runs over, the one named last changes fastest.
Arguments:
- obs_source: int32 [524288], P(('sky', 'tm')), may hold values from 0 to 1023
- obs_knot: int32 [524288], P(('sky', 'tm')), may hold values from 0 to 4095, as said below
- obs_count: int32 [128], P(('sky', 'tm')), may hold values from 256 to 4096, as said below
- src_design: float32 [5, 524288], P(None, ('sky', 'tm')), may hold values from -3 to 3
- att_design: float32 [4, 524288], P(None, ('sky', 'tm')), may hold values from -6 to 6
- obs_phase: float32 [524288], P(('sky', 'tm')), may hold values from 0 to 1
- obs_value: float32 [524288], P(('sky', 'tm')), may hold values from -6 to 6
- src_prior: float32 [5, 16384], P(None, 'sky'), may hold values from 1 to 16
Outputs:
- att_solution: float32 [4, 8, 4096], P(None, 'tm', 'sky')
- att_residual: float32 [4, 8, 4096], P(None, 'tm', 'sky')
- source_solution: float32 [5, 16384], P(None, 'sky')
The draws below stay inside these ranges and needn't reach their ends.
Inputs may be any that keep to these rules, and one draw needn't show every extreme that they name: Block b holds the 4096 observation slots o with o // 4096 = b; with i = b // 8 its sources are the sources i * 1024 + obs_source. With j = b % 8 for the observation's block b, its four spline knots are j * 4096 + obs_knot and the next three. In every block, each range of 256 values r * 256 to r * 256 + 255 of obs_knot holds exactly 256 of the block's slots. `obs_count`: each count is 4096 divided by 1, 2, 4, 8 or 16; the live slots of a block are its first ones; some block is full.
All inputs are finite; a program needn't handle non-finite values.
Results may differ from the reference program's by a relative error of at most 0.0001.
Values sent between devices are 32-bit elements; how exact they have to be, the bound alone decides.
No kernel may reach another device: no remote copies, remote signals or barrier semaphores. Data moves between devices by JAX's collectives and lax.ppermute only.
A program may use at most 64 MiB of HBM per device.

```python
import math
import jax
import jax.numpy as jnp
from jax import lax

PARAMS = 5
COMP = 4
ITERS = 2
SRC_DEV = 1024
OBS_DEV = 4096
KN_DEV = 256
KSEG = 4096
KNOTS = 32768
SOURCES = 16384
BLOCKS = 128
OBS = 524288
N_TM = 8


def draw_obs_count(key, part):
    shifts = jax.random.randint(jax.random.fold_in(key, 11), (BLOCKS,), 0, 5)
    fullest = jax.random.randint(jax.random.fold_in(key, 12), (), 0, BLOCKS)
    shifts = jnp.where(jnp.arange(BLOCKS) == fullest, 0, shifts).astype(jnp.int32)
    return jnp.right_shift(jnp.full((BLOCKS,), OBS_DEV, jnp.int32), shifts)


def shuffle(block_key):
    return jax.random.permutation(block_key, OBS_DEV)


def draw_obs_knot(key, part):
    span_count = KSEG // KN_DEV
    block_keys = jax.random.split(jax.random.fold_in(key, 21), BLOCKS)
    orders = jax.vmap(shuffle)(block_keys)
    owners = (orders % span_count).reshape(-1)
    offsets = jax.random.randint(jax.random.fold_in(key, 22), (OBS,), 0, KN_DEV)
    return (owners * KN_DEV + offsets).astype(jnp.int32)


def plant(entries, key, smallest, high):
    spot = [jax.random.randint(jax.random.fold_in(key, axis), (), 0, length) for axis, length in enumerate(entries.shape)]
    widest = entries.shape.index(max(entries.shape))
    neighbour = spot[:widest] + [(spot[widest] + 1) % entries.shape[widest]] + spot[widest + 1:]
    return entries.at[tuple(spot)].set(smallest).at[tuple(neighbour)].set(high)


def shard_levels(own_key, shape, pieces, least, high):
    loudness = 1.0
    for dim, shards_of in pieces:
        heights = jax.random.uniform(jax.random.fold_in(jax.random.fold_in(own_key, 6), dim), (shards_of,), jnp.float32, least / len(pieces), high / len(pieces))
        loudness = loudness * jnp.repeat(jnp.exp(heights), shape[dim] // shards_of).reshape((-1,) + (1,) * (len(shape) - 1 - dim))
    return loudness


def scatter_about(stream_key, shape, width, reach, pieces=(), kind=jnp.bfloat16):
    loudness = shard_levels(stream_key, shape, pieces, -0.22, 0.18) if pieces else 1.0
    values = jax.random.normal(stream_key, shape, jnp.float32) * width * loudness
    return jnp.minimum(jnp.maximum(values, -reach), reach).astype(kind)


def setup_inputs(seed: int = 0) -> dict:
    splits = jax.random.split(jax.random.key(seed), 9)
    return {
        "obs_source": plant(jax.random.randint(splits[0], (OBS,), 0, SRC_DEV), jax.random.fold_in(splits[0], 1), 0, SRC_DEV - 1).astype(jnp.int32),
        "obs_knot": draw_obs_knot(jax.random.fold_in(splits[8], 71), 0),
        "obs_count": draw_obs_count(jax.random.fold_in(splits[8], 71), 0),
        "src_design": scatter_about(splits[3], (PARAMS, OBS), 0.5, 3.0, ((1, 128),), jnp.float32),
        "att_design": scatter_about(splits[4], (COMP, OBS), 1.0, 6.0, ((1, 128),), jnp.float32),
        "obs_phase": jnp.clip(1.0 * jax.random.uniform(splits[5], (OBS,), jnp.float32) ** shard_levels(splits[5], (OBS,), ((0, 128),), -0.2, 0.2), 0.0, 1.0),
        "obs_value": scatter_about(splits[6], (OBS,), 1.0, 6.0, ((0, 128),), jnp.float32),
        "src_prior": jnp.clip(jnp.exp(math.log(16.0) - 2.7725887 * jax.random.uniform(splits[7], (PARAMS, SOURCES), jnp.float32) ** shard_levels(splits[7], (PARAMS, SOURCES), ((1, 16),), -0.2, 0.2)), 1.0, 16.0),
    }


damping = 0.5
entry_pairs = [(row_at, col_at) for row_at in range(5) for col_at in range(row_at + 1)]

def spline_taps(phase):
    squared = phase * phase
    cubed = squared * phase
    rest = 1.0 - phase
    return (rest * rest * rest / 6.0, (3.0 * cubed - 6.0 * squared + 4.0) / 6.0, (-3.0 * cubed + 3.0 * squared + 3.0 * phase + 1.0) / 6.0, cubed / 6.0)

def factorize(normal):
    factor = {}
    for row_at in range(5):
        for col_at in range(row_at + 1):
            running = normal[row_at, col_at]
            for inner_at in range(col_at):
                running = running - factor[row_at, inner_at] * factor[col_at, inner_at]
            if row_at == col_at:
                factor[row_at, row_at] = jnp.sqrt(running)
            else:
                factor[row_at, col_at] = running / factor[col_at, col_at]
    return factor

def chol_solve(factor, target):
    forward = []
    for row_at in range(5):
        running = target[row_at]
        for inner_at in range(row_at):
            running = running - factor[row_at, inner_at] * forward[inner_at]
        forward.append(running / factor[row_at, row_at])
    result = [None] * 5
    for row_at in reversed(range(5)):
        running = forward[row_at]
        for inner_at in range(row_at + 1, 5):
            running = running - factor[inner_at, row_at] * result[inner_at]
        result[row_at] = running / factor[row_at, row_at]
    return jnp.stack(result)

def source_total(source, rows, count):
    return jnp.zeros((rows.shape[0], count), jnp.float32).at[:, source].add(rows)

def knot_values(padded, knot, design, tap_weights):
    summed = jnp.zeros(knot.shape, jnp.float32)
    for tap_at in range(4):
        picked = jnp.take(padded, knot + tap_at, axis=1)
        summed = summed + tap_weights[tap_at] * lax.optimization_barrier(jnp.sum(design * picked, axis=0))
    return summed

def knot_total(knot, design, tap_weights, weight_vec, extent):
    summed = jnp.zeros((design.shape[0], extent + 3), jnp.float32)
    for tap_at in range(4):
        summed = summed.at[:, knot + tap_at].add(design * (tap_weights[tap_at] * weight_vec))
    return summed

def eliminate(factor, source, design, values_obs, source_sums):
    solved = chol_solve(factor, [source_sums[row_at] for row_at in range(5)])
    fitted = lax.optimization_barrier(jnp.sum(design * jnp.take(solved, source, axis=1), axis=0))
    return values_obs - fitted

def reference(obs_source, obs_knot, obs_count, src_design, att_design, obs_phase, obs_value, src_prior):
    live_mask = (jnp.arange(OBS_DEV, dtype=jnp.int32)[None, :] < obs_count[:, None]).astype(jnp.float32).reshape(-1)
    block_of = jnp.arange(OBS, dtype=jnp.int32) // OBS_DEV
    source = (block_of // N_TM * SRC_DEV + obs_source).astype(jnp.int32)
    knot = (block_of % N_TM * KSEG + obs_knot).astype(jnp.int32)
    src_rows = src_design * live_mask
    att_rows = att_design * live_mask
    observed = obs_value * live_mask
    tap_weights = spline_taps(obs_phase)
    products = jnp.stack([src_rows[row_at] * src_rows[col_at] for row_at, col_at in entry_pairs] + [src_rows[row_at] * observed for row_at in range(5)])
    sums = source_total(source, products, SOURCES)
    normal = {}
    for entry_at, pair in enumerate(entry_pairs):
        normal[pair] = sums[entry_at] + (src_prior[pair[0]] if pair[0] == pair[1] else 0.0)
    factor = factorize(normal)

    def reduced(values_obs, totals):
        cleaned = eliminate(factor, source, src_rows, values_obs, totals)
        return knot_total(knot, att_rows, tap_weights, cleaned, KNOTS)[:, :KNOTS]

    def along_knots(field):
        padded = jnp.concatenate([field, jnp.zeros((4, 3), jnp.float32)], axis=1)
        return knot_values(padded, knot, att_rows, tap_weights)
    residual = reduced(observed, sums[15:])
    solution = jnp.zeros_like(residual)
    direction = residual
    norm_now = jnp.sum(residual * residual)
    for repeat in range(ITERS):
        image_obs = along_knots(direction)
        mapped = reduced(image_obs, source_total(source, src_rows * image_obs, SOURCES)) + damping * direction
        alpha_step = norm_now / jnp.sum(direction * mapped)
        solution = solution + alpha_step * direction
        residual = residual - alpha_step * mapped
        norm_next = jnp.sum(residual * residual)
        direction = residual + norm_next / norm_now * direction
        norm_now = norm_next
    fitted = observed - along_knots(solution)
    source_solution = chol_solve(factor, [row for row in source_total(source, src_rows * fitted, SOURCES)])
    return (solution.reshape(4, N_TM, KSEG), residual.reshape(4, N_TM, KSEG), source_solution)
```

```python
import functools

import jax
import jax.numpy as jnp
from jax import lax
from jax.experimental import pallas as pl
from jax.experimental.pallas import tpu as pltpu
from jax.sharding import Mesh
from jax.sharding import PartitionSpec as P

SKY = ("sky_0", "sky_1")
TM = ("tm_0", "tm_1")
SKY_TM = ("sky_0", "sky_1", "tm_0", "tm_1")

OBS_DEV = 4096
CHUNK = 1024
damping = 0.5
entry_pairs = [(row_at, col_at) for row_at in range(5) for col_at in range(row_at + 1)]


f32 = jnp.float32
bf16 = jnp.bfloat16


def split_rows(value):
    first = value.astype(bf16)
    rest = value - first.astype(f32)
    second = rest.astype(bf16)
    third = (rest - second.astype(f32)).astype(bf16)
    return jnp.concatenate([first, second, third], axis=0)


def join_rows(stacked):
    rows = stacked.shape[0] // 3
    return stacked[:rows] + (stacked[rows : 2 * rows] + stacked[2 * rows :])


def dot_nt(left, right):
    return lax.dot_general(left, right, (((1,), (1,)), ((), ())), preferred_element_type=f32)


def dot_nn(left, right):
    return lax.dot_general(left, right, (((1,), (0,)), ((), ())), preferred_element_type=f32)


def chunks():
    return [slice(start, start + CHUNK) for start in range(0, OBS_DEV, CHUNK)]


def four(refs):
    own, one, two, three = (ref[...] for ref in refs)
    return (own + two) + (one + three)


def lanes_from(start, rows):
    return lax.broadcasted_iota(jnp.int32, (rows, CHUNK), 1) + start


def source_kernel(count_ref, source_ref, g_ref, y_ref, hot_ref, spread_ref, y_live_ref, sums_ref):
    total = jnp.zeros((480, 128), f32)
    for at in chunks():
        live = lanes_from(at.start, 1) < count_ref[0]
        source = source_ref[:, at]
        hot = jnp.where(lax.broadcasted_iota(jnp.int32, (128, CHUNK), 0) == (source & 127), 1.0, 0.0).astype(bf16)
        hot_ref[:, at] = hot
        mark = jnp.where(live, source >> 7, -1)
        chosen = jnp.where(lax.broadcasted_iota(jnp.int32, (8, CHUNK), 0) == mark, 1.0, 0.0)
        g = [g_ref[j : j + 1, at] for j in range(5)]
        y = y_ref[:, at]
        y_live_ref[:, at] = jnp.where(live, y, 0.0)
        spread = [chosen * g[j] for j in range(5)]
        for j in range(5):
            spread_ref[8 * j : 8 * j + 8, at] = spread[j]
        rows = [spread[r] * g[c] for r, c in entry_pairs] + [spread[j] * y for j in range(5)]
        total = total + dot_nt(split_rows(jnp.concatenate(rows, axis=0)), hot)
    sums_ref[...] = join_rows(total)


def knot_kernel(count_ref, last_ref, knot_ref, h_ref, phase_ref, hot_ref, spread_ref):
    upper = lax.broadcasted_iota(jnp.int32, (8, CHUNK), 0) >> 2
    for at in chunks():
        live = lanes_from(at.start, 1) < count_ref[0]
        knot = knot_ref[:, at]
        high = knot >> 4
        hot_ref[:, at] = jnp.where(lax.broadcasted_iota(jnp.int32, (256, CHUNK), 0) == high, 1.0, 0.0).astype(bf16)
        h = jnp.where(live, h_ref[:, at], 0.0)
        h = jnp.concatenate([h, h], axis=0)
        phase = phase_ref[:, at]
        squared = phase * phase
        cubed = squared * phase
        rest = 1.0 - phase
        taps = (
            rest * rest * rest / 6.0,
            (3.0 * cubed - 6.0 * squared + 4.0) / 6.0,
            (-3.0 * cubed + 3.0 * squared + 3.0 * phase + 1.0) / 6.0,
            cubed / 6.0,
        )
        taps = [jnp.broadcast_to(tap, (8, CHUNK)) for tap in taps]
        ahead = upper - (knot & 15)
        kept = jnp.where((high == 255) & (last_ref[0] == 1), 0.0, 1.0)
        for q in range(10):
            gap = ahead + 2 * q
            weight = jnp.where(gap == 0, taps[0], 0.0)
            for m in range(1, 4):
                weight = jnp.where(gap == m, taps[m], weight)
            if q >= 8:
                weight = weight * kept
            spread_ref[8 * q : 8 * q + 8, at] = weight * h


def tile(value, at):
    return value[8 * at : 8 * at + 8]


def factor_of(value):
    return {pair: tile(value, at) for at, pair in enumerate(entry_pairs)}


def factorize(normal):
    factor = {}
    for row_at in range(5):
        for col_at in range(row_at + 1):
            running = normal[row_at, col_at]
            for inner_at in range(col_at):
                running = running - factor[row_at, inner_at] * factor[col_at, inner_at]
            if row_at == col_at:
                factor[row_at, row_at] = jnp.sqrt(running)
            else:
                factor[row_at, col_at] = running / factor[col_at, col_at]
    return factor


def chol_solve(factor, target):
    forward = []
    for row_at in range(5):
        running = target[row_at]
        for inner_at in range(row_at):
            running = running - factor[row_at, inner_at] * forward[inner_at]
        forward.append(running / factor[row_at, row_at])
    result = [None] * 5
    for row_at in reversed(range(5)):
        running = forward[row_at]
        for inner_at in range(row_at + 1, 5):
            running = running - factor[inner_at, row_at] * result[inner_at]
        result[row_at] = running / factor[row_at, row_at]
    return result


def eliminate_and_spread(solved, values_ref, source_hot_ref, source_spread_ref, knot_hot_ref, knot_spread_ref):
    solved = split_rows(jnp.concatenate(solved, axis=0))
    total = jnp.zeros((240, 256), f32)
    for at in chunks():
        picked = join_rows(dot_nn(solved, source_hot_ref[:, at]))
        fitted = jnp.sum(picked * source_spread_ref[:, at], axis=0, keepdims=True)
        cleaned = values_ref[:, at] - fitted
        total = total + dot_nt(split_rows(knot_spread_ref[:, at] * cleaned), knot_hot_ref[:, at])
    return join_rows(total)


def put_knots(total, energy, knots_ref, edge_ref):
    knots_ref[0:72] = total[0:72]
    if energy is None:
        tail = total[76:80]
    else:
        tail = jnp.concatenate([energy[0:4], energy[4:8]], axis=1)
    knots_ref[72:80] = jnp.concatenate([total[72:76], tail], axis=0)
    lane = lax.broadcasted_iota(jnp.int32, (16, 128), 1)
    edge_ref[...] = jnp.where(lane == 127, total[64:80, 128:256], jnp.where(lane == 0, total[0:16, 0:128], 0.0))


def first_kernel(own, one, two, three, prior_ref, y_ref, source_hot, source_spread, knot_hot, knot_spread, knots_ref, edge_ref, factor_ref, rhs_ref):
    sums = four((own, one, two, three))
    normal = factor_of(sums)
    for j in range(5):
        prior = jnp.concatenate([prior_ref[j : j + 1, 128 * a : 128 * a + 128] for a in range(8)], axis=0)
        normal[j, j] = normal[j, j] + prior
    factor = factorize(normal)
    for at, pair in enumerate(entry_pairs):
        factor_ref[8 * at : 8 * at + 8] = factor[pair]
    rhs_ref[...] = sums[120:160]
    solved = chol_solve(factor, [tile(sums, 15 + j) for j in range(5)])
    total = eliminate_and_spread(solved, y_ref, source_hot, source_spread, knot_hot, knot_spread)
    put_knots(total, None, knots_ref, edge_ref)


def back_kernel(energy_at, own, one, two, three, factor_ref, values_ref, source_hot, source_spread, knot_hot, knot_spread, knots_ref, edge_ref, sums_ref):
    sums = four((own, one, two, three))
    sums_ref[...] = sums
    target = [tile(sums, j) for j in range(5)]
    solved = chol_solve(factor_of(factor_ref[...]), target)
    energy = tile(sums, energy_at)
    for j in range(5):
        energy = energy - target[j] * solved[j]
    total = eliminate_and_spread(solved, values_ref, source_hot, source_spread, knot_hot, knot_spread)
    put_knots(total, energy, knots_ref, edge_ref)


def assembled(knots):
    lane = lax.broadcasted_iota(jnp.int32, (16, 256), 1)
    row = lax.broadcasted_iota(jnp.int32, (16, 256), 0)
    beyond = jnp.where(row < 12, knots[64:80], 0.0)
    low = knots[0:16] + jnp.where(lane == 0, 0.0, jnp.concatenate([beyond[:, 255:256], beyond[:, 0:255]], axis=1))
    following = jnp.concatenate([low[:, 1:256], low[:, 0:1]], axis=1)
    high = jnp.where(row < 12, jnp.where(lane == 255, beyond, following), 0.0)
    return jnp.concatenate([low, knots[16:64], high], axis=0)


def energy_of(knots):
    return jnp.sum(knots[76:80])


def folded(left, right):
    product = left[0:64] * right[0:64]
    product = product[:, 0:128] + product[:, 128:256]
    return functools.reduce(jnp.add, [tile(product, at) for at in range(8)])


def gather_and_sum(field, source_hot_ref, source_spread_ref, knot_hot_ref, knot_spread_ref, image_ref):
    parts = split_rows(field)
    total = jnp.zeros((120, 128), f32)
    square = jnp.zeros((1, 128), f32)
    for at in chunks():
        picked = join_rows(dot_nn(parts, knot_hot_ref[:, at]))
        image = jnp.sum(picked * knot_spread_ref[:, at], axis=0, keepdims=True)
        image_ref[:, at] = image
        for start in range(0, CHUNK, 128):
            piece = image[:, start : start + 128]
            square = square + piece * piece
        total = total + dot_nt(split_rows(source_spread_ref[:, at] * image), source_hot_ref[:, at])
    return join_rows(total), jnp.concatenate([square, jnp.zeros((7, 128), f32)], axis=0)


def start_kernel(own, one, two, three, source_hot, source_spread, knot_hot, knot_spread, sums_ref, image_ref, field_ref):
    residual = assembled(four((own, one, two, three)))
    field_ref[...] = residual
    sums, square = gather_and_sum(residual, source_hot, source_spread, knot_hot, knot_spread, image_ref)
    sums_ref[...] = jnp.concatenate([sums, square, folded(residual, residual)], axis=0)


def next_kernel(own, one, two, three, residual_ref, before_ref, source_hot, source_spread, knot_hot, knot_spread, sums_ref, image_ref, mapped_ref, field_ref, scalar_ref):
    knots = four((own, one, two, three))
    direction = residual_ref[...]
    mapped = assembled(knots) + damping * direction
    norm_now = jnp.sum(before_ref[48:56])
    product = energy_of(knots) + damping * norm_now
    residual = direction - (norm_now / product) * mapped
    mapped_ref[...] = mapped
    field_ref[...] = residual
    scalar_ref[...] = jnp.zeros((8, 128), f32) + product
    sums, square = gather_and_sum(residual, source_hot, source_spread, knot_hot, knot_spread, image_ref)
    sums_ref[...] = jnp.concatenate([sums, square, folded(residual, residual), folded(residual, mapped)], axis=0)


def last_kernel(place_ref, own, one, two, three, start_ref, mapped_ref, residual_ref, scalar_ref, before_ref, after_ref, factor_ref, rhs_ref, solution_ref, left_ref, source_ref):
    knots = four((own, one, two, three))
    residual = residual_ref[0:64]
    image = assembled(knots)[0:64] + damping * residual
    norm_first = jnp.sum(before_ref[48:56])
    product_first = jnp.max(scalar_ref[...])
    alpha_first = norm_first / product_first
    norm_now = jnp.sum(after_ref[48:56])
    crossed = jnp.sum(after_ref[56:64])
    beta = norm_now / norm_first
    product = energy_of(knots) + damping * norm_now + beta * (2.0 * crossed + beta * product_first)
    alpha = norm_now / product
    from_start = alpha_first + alpha * beta
    solution = from_start * start_ref[0:64] + alpha * residual
    left = residual - alpha * (image + beta * mapped_ref[0:64])
    both = split_rows(jnp.concatenate([solution, left], axis=0))
    row = lax.broadcasted_iota(jnp.int32, (256, 256), 0)
    lane = lax.broadcasted_iota(jnp.int32, (256, 256), 1)
    chosen = jnp.where(row == place_ref[0] * 16 + (lane >> 4), 1.0, 0.0).astype(bf16)
    picked = join_rows(dot_nn(both, chosen))
    low = lax.broadcasted_iota(jnp.int32, (8, 256), 1) & 15
    upper = lax.broadcasted_iota(jnp.int32, (8, 256), 0) >> 2
    for at, ref in enumerate((solution_ref, left_ref)):
        own_rows = jnp.zeros((8, 256), f32)
        for q in range(8):
            own_rows = jnp.where(low == upper + 2 * q, tile(picked, 8 * at + q), own_rows)
        ref[...] = own_rows[0:4] + own_rows[4:8]
    target = [tile(rhs_ref, j) - from_start * tile(before_ref, j) - alpha * tile(after_ref, j) for j in range(5)]
    solved = chol_solve(factor_of(factor_ref[...]), target)
    for j in range(5):
        for a in range(8):
            source_ref[j : j + 1, 128 * a : 128 * a + 128] = solved[j][a : a + 1]


VMEM = pl.BlockSpec(memory_space=pltpu.VMEM)
SMEM = pl.BlockSpec(memory_space=pltpu.SMEM)


def call(kernel, name, outs, *operands, scalars=0):
    specs = [SMEM] * scalars + [VMEM] * (len(operands) - scalars)
    shapes = [jax.ShapeDtypeStruct(shape, dtype) for shape, dtype in outs]
    return pl.pallas_call(
        kernel,
        out_shape=shapes,
        in_specs=specs,
        out_specs=[VMEM] * len(outs),
        compiler_params=pltpu.CompilerParams(vmem_limit_bytes=32 * 1024 * 1024),
        name=name,
    )(*operands)


def ring_parts(value, axis):
    count = lax.axis_size(axis)
    return [value] + [
        lax.ppermute(value, axis, [(at, (at + step) % count) for at in range(count)]) for step in (1, 2, 3)
    ]


def tm_parts(value):
    value = value + lax.ppermute(value, "tm_1", [(0, 1), (1, 0)])
    return ring_parts(value, "tm_0")


def sky_parts(knots, edge):
    count = lax.axis_size(TM)
    at = lax.axis_index(TM)
    twin = lax.ppermute(edge, "tm_1", [(0, 1), (1, 0)])
    swaps = [(low, low + 1) for low in range(1, count - 1, 2)]
    other = lax.ppermute(edge, TM, swaps + [(high, low) for low, high in swaps])
    odd = at % 2 == 1
    earlier = jnp.where(odd, twin, other)[:, 127]
    later = jnp.where(odd, other, twin)[:, 0]
    row = lax.broadcasted_iota(jnp.int32, (80, 256), 0)
    lane = lax.broadcasted_iota(jnp.int32, (80, 256), 1)
    keep_low = jnp.arange(16) < 12
    keep_high = (jnp.arange(16) < 12) & (at < count - 1)
    low = jnp.concatenate([jnp.where(keep_low, earlier, 0.0), jnp.zeros((64,), f32)])
    high = jnp.concatenate([jnp.zeros((64,), f32), jnp.where(keep_high, later, 0.0)])
    knots = knots + jnp.where(lane == 0, low[:, None], 0.0) + jnp.where(lane == 255, high[:, None], 0.0)
    own, one, two, three = ring_parts(knots, "sky_1")
    return ring_parts((own + two) + (one + three), "sky_0")


def shards(obs_source, obs_knot, obs_count, src_design, att_design, obs_phase, obs_value, src_prior):
    last = (lax.axis_index(TM) == lax.axis_size(TM) - 1).astype(jnp.int32).reshape(1)
    place = lax.axis_index(SKY).astype(jnp.int32).reshape(1)
    line = lambda value: value.reshape(1, OBS_DEV)
    source_hot, source_spread, y_live, sums = call(
        source_kernel,
        "source_sums",
        [((128, OBS_DEV), bf16), ((40, OBS_DEV), f32), ((1, OBS_DEV), f32), ((160, 128), f32)],
        obs_count, line(obs_source), src_design, line(obs_value),
        scalars=1,
    )
    parts = tm_parts(sums)
    knot_hot, knot_spread = call(
        knot_kernel,
        "knot_spread",
        [((256, OBS_DEV), bf16), ((80, OBS_DEV), f32)],
        obs_count, last, line(obs_knot), att_design, line(obs_phase),
        scalars=2,
    )
    maps = (source_hot, source_spread, knot_hot, knot_spread)
    knots_out = [((80, 256), f32), ((16, 128), f32)]
    knots, edge, factor, rhs = call(
        first_kernel, "first", knots_out + [((120, 128), f32), ((40, 128), f32)], *parts, src_prior, y_live, *maps
    )
    parts = sky_parts(knots, edge)
    sums, image, start = call(
        start_kernel, "start", [((56, 128), f32), ((1, OBS_DEV), f32), ((80, 256), f32)], *parts, *maps
    )
    parts = tm_parts(sums)
    knots, edge, before = call(
        functools.partial(back_kernel, 5), "back", knots_out + [((56, 128), f32)], *parts, factor, image, *maps
    )
    parts = sky_parts(knots, edge)
    sums, image, mapped, residual, scalar = call(
        next_kernel,
        "next",
        [((64, 128), f32), ((1, OBS_DEV), f32), ((80, 256), f32), ((80, 256), f32), ((8, 128), f32)],
        *parts, start, before, *maps,
    )
    parts = tm_parts(sums)
    knots, edge, after = call(
        functools.partial(back_kernel, 5), "back_again", knots_out + [((64, 128), f32)], *parts, factor, image, *maps
    )
    parts = sky_parts(knots, edge)
    solution, left, source_solution = call(
        last_kernel,
        "last",
        [((4, 256), f32), ((4, 256), f32), ((5, 1024), f32)],
        place, *parts, start, mapped, residual, scalar, before, after, factor, rhs,
        scalars=1,
    )
    return (solution[:, None, :], left[:, None, :], source_solution)


def solution(mesh):
    torus = Mesh(mesh.devices.reshape(4, 4, 4, 2), SKY_TM)
    placed = (
        P(SKY_TM),
        P(SKY_TM),
        P(SKY_TM),
        P(None, SKY_TM),
        P(None, SKY_TM),
        P(SKY_TM),
        P(SKY_TM),
        P(None, SKY),
    )
    return jax.shard_map(
        shards,
        mesh=torus,
        in_specs=placed,
        out_specs=(P(None, TM, SKY), P(None, TM, SKY), P(None, SKY)),
        check_vma=False,
    )
```

```python
import functools

import jax
import jax.numpy as jnp
from jax import lax
from jax.experimental import pallas as pl
from jax.experimental.pallas import tpu as pltpu
from jax.sharding import Mesh
from jax.sharding import PartitionSpec as P

SKY = ("sky_0", "sky_1")
TM = ("tm_0", "tm_1")
SKY_TM = ("sky_0", "sky_1", "tm_0", "tm_1")

OBS_DEV = 4096
CHUNK = 1024
damping = 0.5
entry_pairs = [(row_at, col_at) for row_at in range(5) for col_at in range(row_at + 1)]


f32 = jnp.float32
bf16 = jnp.bfloat16


def split_rows(value):
    first = value.astype(bf16)
    rest = value - first.astype(f32)
    second = rest.astype(bf16)
    third = (rest - second.astype(f32)).astype(bf16)
    return jnp.concatenate([first, second, third], axis=0)


def join_rows(stacked):
    rows = stacked.shape[0] // 3
    return stacked[:rows] + (stacked[rows : 2 * rows] + stacked[2 * rows :])


def dot_nt(left, right):
    return lax.dot_general(left, right, (((1,), (1,)), ((), ())), preferred_element_type=f32)


def dot_nn(left, right):
    return lax.dot_general(left, right, (((1,), (0,)), ((), ())), preferred_element_type=f32)


def chunks():
    return [slice(start, start + CHUNK) for start in range(0, OBS_DEV, CHUNK)]


def four(refs):
    own, one, two, three = (ref[...] for ref in refs)
    return (own + two) + (one + three)


def lanes_from(start, rows):
    return lax.broadcasted_iota(jnp.int32, (rows, CHUNK), 1) + start


SOURCE_SPREAD = slice(0, 40)
KNOT_SPREAD = slice(40, 120)
IMAGE = slice(120, 121)
SOURCE_LANE = slice(121, 122)
KNOT_LANE = slice(122, 123)
START, MAPPED, RESIDUAL = (slice(at, at + 256) for at in (0, 256, 512))
FACTOR_A, FACTOR_B, BEFORE, AFTER, SCALAR = (slice(at, at + 128) for at in (768, 896, 1024, 1152, 1280))
WORK = ((128, OBS_DEV), f32)
STATE = ((80, 1408), f32)


def put(state, lanes, start, value):
    state[start : start + value.shape[0], lanes] = value


def get(state, lanes, start, rows):
    return state[start : start + rows, lanes]


def row_numbers(rows):
    return lax.broadcasted_iota(jnp.int32, (rows, CHUNK), 0).astype(f32).astype(bf16)


def hot_rows(numbers, lane_row):
    wanted = jnp.broadcast_to(lane_row, numbers.shape).astype(bf16)
    return jnp.where(numbers == wanted, jnp.ones_like(numbers), jnp.zeros_like(numbers))


def open_kernel(state):
    state[0:8, 0:128] = jnp.zeros((8, 128), f32)


def source_kernel(count_ref, first_ref, source_ref, g_ref, y_ref, prior_ref, _state, work, sums_ref, state):
    numbers = row_numbers(128)
    total = jnp.zeros((480, 128), f32)
    for at in chunks():
        live = lanes_from(at.start, 1) < count_ref[0]
        source = source_ref[:, at]
        lane = (source & 127).astype(f32)
        work[SOURCE_LANE, at] = lane
        mark = jnp.where(live, source >> 7, -1)
        chosen = jnp.where(lax.broadcasted_iota(jnp.int32, (8, CHUNK), 0) == mark, 1.0, 0.0)
        g = [g_ref[j : j + 1, at] for j in range(5)]
        y = y_ref[:, at]
        work[IMAGE, at] = y
        spread = [chosen * g[j] for j in range(5)]
        for j in range(5):
            work[8 * j : 8 * j + 8, at] = spread[j]
        rows = [spread[r] * g[c] for r, c in entry_pairs] + [spread[j] * y for j in range(5)]
        total = total + dot_nt(split_rows(jnp.concatenate(rows, axis=0)), hot_rows(numbers, lane))
    sums_ref[...] = join_rows(total)
    once = jnp.where(first_ref[0] == 1, 1.0, 0.0)
    for at, (row_at, col_at) in enumerate(entry_pairs):
        if row_at == col_at:
            prior = jnp.concatenate([prior_ref[row_at : row_at + 1, 128 * a : 128 * a + 128] for a in range(8)], axis=0)
            sums_ref[8 * at : 8 * at + 8] += prior * once


def knot_kernel(count_ref, last_ref, knot_ref, h_ref, phase_ref, _work, work):
    upper = lax.broadcasted_iota(jnp.int32, (8, CHUNK), 0) >> 2
    for at in chunks():
        live = lanes_from(at.start, 1) < count_ref[0]
        knot = knot_ref[:, at]
        high = knot >> 4
        work[KNOT_LANE, at] = high.astype(f32)
        h = jnp.where(live, h_ref[:, at], 0.0)
        h = jnp.concatenate([h, h], axis=0)
        phase = phase_ref[:, at]
        squared = phase * phase
        cubed = squared * phase
        rest = 1.0 - phase
        taps = (
            rest * rest * rest / 6.0,
            (3.0 * cubed - 6.0 * squared + 4.0) / 6.0,
            (-3.0 * cubed + 3.0 * squared + 3.0 * phase + 1.0) / 6.0,
            cubed / 6.0,
        )
        taps = [jnp.broadcast_to(tap, (8, CHUNK)) for tap in taps]
        ahead = upper - (knot & 15)
        kept = jnp.where((high == 255) & (last_ref[0] == 1), 0.0, 1.0)
        for q in range(10):
            gap = ahead + 2 * q
            weight = jnp.where(gap == 0, taps[0], 0.0)
            for m in range(1, 4):
                weight = jnp.where(gap == m, taps[m], weight)
            if q >= 8:
                weight = weight * kept
            row = KNOT_SPREAD.start + 8 * q
            work[row : row + 8, at] = weight * h


def tile(value, at):
    return value[8 * at : 8 * at + 8]


def factor_of(value):
    return {pair: tile(value, at) for at, pair in enumerate(entry_pairs)}


def factorize(normal):
    factor = {}
    for row_at in range(5):
        for col_at in range(row_at + 1):
            running = normal[row_at, col_at]
            for inner_at in range(col_at):
                running = running - factor[row_at, inner_at] * factor[col_at, inner_at]
            if row_at == col_at:
                factor[row_at, row_at] = 1.0 / jnp.sqrt(running)
            else:
                factor[row_at, col_at] = running * factor[col_at, col_at]
    return factor


def chol_solve(factor, target):
    forward = []
    for row_at in range(5):
        running = target[row_at]
        for inner_at in range(row_at):
            running = running - factor[row_at, inner_at] * forward[inner_at]
        forward.append(running * factor[row_at, row_at])
    result = [None] * 5
    for row_at in reversed(range(5)):
        running = forward[row_at]
        for inner_at in range(row_at + 1, 5):
            running = running - factor[inner_at, row_at] * result[inner_at]
        result[row_at] = running * factor[row_at, row_at]
    return result


def eliminate_and_spread(solved, work):
    solved = split_rows(jnp.concatenate(solved, axis=0))
    source_numbers, knot_numbers = row_numbers(128), row_numbers(256)
    total = jnp.zeros((240, 256), f32)
    for at in chunks():
        picked = join_rows(dot_nn(solved, hot_rows(source_numbers, work[SOURCE_LANE, at])))
        fitted = jnp.sum(picked * work[SOURCE_SPREAD, at], axis=0, keepdims=True)
        cleaned = work[IMAGE, at] - fitted
        total = total + dot_nt(split_rows(work[KNOT_SPREAD, at] * cleaned), hot_rows(knot_numbers, work[KNOT_LANE, at]))
    return join_rows(total)


def put_knots(total, energy, knots_ref, edge_ref):
    knots_ref[0:72] = total[0:72]
    if energy is None:
        tail = total[76:80]
    else:
        tail = jnp.concatenate([energy[0:4], energy[4:8]], axis=1)
    knots_ref[72:80] = jnp.concatenate([total[72:76], tail], axis=0)
    lane = lax.broadcasted_iota(jnp.int32, (16, 128), 1)
    edge_ref[...] = jnp.where(lane == 127, total[64:80, 128:256], jnp.where(lane == 0, total[0:16, 0:128], 0.0))


def first_kernel(own, one, two, three, _work, _state, knots_ref, edge_ref, work, state):
    sums = four((own, one, two, three))
    factor = factorize(factor_of(sums))
    stacked = jnp.concatenate([factor[pair] for pair in entry_pairs], axis=0)
    put(state, FACTOR_A, 0, stacked[0:80])
    put(state, FACTOR_B, 0, stacked[80:120])
    put(state, FACTOR_B, 40, sums[120:160])
    solved = chol_solve(factor, [tile(sums, 15 + j) for j in range(5)])
    put_knots(eliminate_and_spread(solved, work), None, knots_ref, edge_ref)


def kept_factor(state):
    return factor_of(jnp.concatenate([get(state, FACTOR_A, 0, 80), get(state, FACTOR_B, 0, 40)], axis=0))


def back_kernel(lanes, own, one, two, three, _work, _state, knots_ref, edge_ref, work, state):
    sums = four((own, one, two, three))
    put(state, lanes, 0, sums)
    target = [tile(sums, j) for j in range(5)]
    solved = chol_solve(kept_factor(state), target)
    energy = tile(sums, 5)
    for j in range(5):
        energy = energy - target[j] * solved[j]
    put_knots(eliminate_and_spread(solved, work), energy, knots_ref, edge_ref)


def edge_kernel(odd_ref, _knots, twin_ref, other_ref, knots_ref):
    odd = odd_ref[0] == 1
    twin, other = twin_ref[...], other_ref[...]
    earlier = pltpu.roll(jnp.where(odd, twin, other), 1, 1)
    later = pltpu.roll(jnp.where(odd, other, twin), 127, 1)
    lane = lax.broadcasted_iota(jnp.int32, (16, 128), 1)
    within = lax.broadcasted_iota(jnp.int32, (16, 128), 0) < 12
    knots_ref[0:16, 0:128] += jnp.where(within & (lane == 0), earlier, 0.0)
    knots_ref[64:80, 128:256] += jnp.where(within & (lane == 127), later, 0.0)


def assembled(knots):
    lane = lax.broadcasted_iota(jnp.int32, (16, 256), 1)
    row = lax.broadcasted_iota(jnp.int32, (16, 256), 0)
    beyond = jnp.where(row < 12, knots[64:80], 0.0)
    low = knots[0:16] + jnp.where(lane == 0, 0.0, pltpu.roll(beyond, 1, 1))
    high = jnp.where(row < 12, jnp.where(lane == 255, beyond, pltpu.roll(low, 255, 1)), 0.0)
    return jnp.concatenate([low, knots[16:64], high], axis=0)


def energy_of(knots):
    return jnp.sum(knots[76:80])


def folded(left, right):
    product = left[0:64] * right[0:64]
    product = product[:, 0:128] + product[:, 128:256]
    return functools.reduce(jnp.add, [tile(product, at) for at in range(8)])


def gather_and_sum(field, work):
    source_numbers, knot_numbers = row_numbers(128), row_numbers(256)
    parts = split_rows(field)
    total = jnp.zeros((120, 128), f32)
    square = jnp.zeros((1, 128), f32)
    for at in chunks():
        picked = join_rows(dot_nn(parts, hot_rows(knot_numbers, work[KNOT_LANE, at])))
        image = jnp.sum(picked * work[KNOT_SPREAD, at], axis=0, keepdims=True)
        work[IMAGE, at] = image
        for start in range(0, CHUNK, 128):
            piece = image[:, start : start + 128]
            square = square + piece * piece
        total = total + dot_nt(split_rows(work[SOURCE_SPREAD, at] * image), hot_rows(source_numbers, work[SOURCE_LANE, at]))
    return join_rows(total), jnp.concatenate([square, jnp.zeros((7, 128), f32)], axis=0)


def start_kernel(own, one, two, three, _work, _state, sums_ref, work, state):
    residual = assembled(four((own, one, two, three)))
    put(state, START, 0, residual)
    sums, square = gather_and_sum(residual, work)
    sums_ref[...] = jnp.concatenate([sums, square, folded(residual, residual)], axis=0)


def next_kernel(own, one, two, three, _work, _state, sums_ref, work, state):
    knots = four((own, one, two, three))
    direction = get(state, START, 0, 80)
    mapped = assembled(knots) + damping * direction
    norm_now = jnp.sum(get(state, BEFORE, 48, 8))
    product = energy_of(knots) + damping * norm_now
    residual = direction - (norm_now / product) * mapped
    put(state, MAPPED, 0, mapped)
    put(state, RESIDUAL, 0, residual)
    put(state, SCALAR, 0, jnp.zeros((8, 128), f32) + product)
    sums, square = gather_and_sum(residual, work)
    sums_ref[...] = jnp.concatenate([sums, square, folded(residual, residual), folded(residual, mapped)], axis=0)


def last_kernel(place_ref, own, one, two, three, state, solution_ref, left_ref, source_ref):
    knots = four((own, one, two, three))
    residual = get(state, RESIDUAL, 0, 64)
    image = assembled(knots)[0:64] + damping * residual
    before, after = get(state, BEFORE, 0, 56), get(state, AFTER, 0, 64)
    norm_first = jnp.sum(before[48:56])
    product_first = jnp.max(get(state, SCALAR, 0, 8))
    alpha_first = norm_first / product_first
    norm_now = jnp.sum(after[48:56])
    crossed = jnp.sum(after[56:64])
    beta = norm_now / norm_first
    product = energy_of(knots) + damping * norm_now + beta * (2.0 * crossed + beta * product_first)
    alpha = norm_now / product
    from_start = alpha_first + alpha * beta
    solution = from_start * get(state, START, 0, 64) + alpha * residual
    left = residual - alpha * (image + beta * get(state, MAPPED, 0, 64))
    both = split_rows(jnp.concatenate([solution, left], axis=0))
    row = lax.broadcasted_iota(jnp.int32, (256, 256), 0)
    lane = lax.broadcasted_iota(jnp.int32, (256, 256), 1)
    chosen = jnp.where(row == place_ref[0] * 16 + (lane >> 4), 1.0, 0.0).astype(bf16)
    picked = join_rows(dot_nn(both, chosen))
    low = lax.broadcasted_iota(jnp.int32, (8, 256), 1) & 15
    upper = lax.broadcasted_iota(jnp.int32, (8, 256), 0) >> 2
    for at, ref in enumerate((solution_ref, left_ref)):
        own_rows = jnp.zeros((8, 256), f32)
        for q in range(8):
            own_rows = jnp.where(low == upper + 2 * q, tile(picked, 8 * at + q), own_rows)
        own_rows = own_rows[0:4] + own_rows[4:8]
        for c in range(4):
            ref[c] = own_rows[c : c + 1]
    rhs = get(state, FACTOR_B, 40, 40)
    target = [tile(rhs, j) - from_start * tile(before, j) - alpha * tile(after, j) for j in range(5)]
    solved = chol_solve(kept_factor(state), target)
    for j in range(5):
        for a in range(8):
            source_ref[j : j + 1, 128 * a : 128 * a + 128] = solved[j][a : a + 1]


VMEM = pl.BlockSpec(memory_space=pltpu.VMEM)
SMEM = pl.BlockSpec(memory_space=pltpu.SMEM)


def call(kernel, name, outs, *operands, scalars=0, aliases=None, work_ahead=0):
    specs = [SMEM] * scalars + [VMEM] * (len(operands) - scalars)
    shapes = [jax.ShapeDtypeStruct(shape, dtype) for shape, dtype in outs]
    return pl.pallas_call(
        kernel,
        out_shape=shapes,
        in_specs=specs,
        out_specs=[VMEM] * len(outs),
        input_output_aliases=aliases or {},
        compiler_params=pltpu.CompilerParams(vmem_limit_bytes=8 * 1024 * 1024),
        cost_estimate=pl.CostEstimate(flops=work_ahead, bytes_accessed=0, transcendentals=0) if work_ahead else None,
        name=name,
    )(*operands)


def ring_parts(value, axis):
    count = lax.axis_size(axis)
    return [value] + [
        lax.ppermute(value, axis, [(at, (at + step) % count) for at in range(count)]) for step in (1, 2, 3)
    ]


def tm_parts(value):
    value = value + lax.ppermute(value, "tm_1", [(0, 1), (1, 0)])
    return ring_parts(value, "tm_0")


def sky_parts(knots, edge, odd):
    count = lax.axis_size(TM)
    twin = lax.ppermute(edge, "tm_1", [(0, 1), (1, 0)])
    swaps = [(low, low + 1) for low in range(1, count - 1, 2)]
    other = lax.ppermute(edge, TM, swaps + [(high, low) for low, high in swaps])
    (knots,) = call(edge_kernel, "edges", [KNOTS], odd, knots, twin, other, scalars=1, aliases={1: 0})
    own, one, two, three = ring_parts(knots, "sky_1")
    return ring_parts((own + two) + (one + three), "sky_0")


KNOTS = ((80, 256), f32)
EDGE = ((16, 128), f32)


def shards(obs_source, obs_knot, obs_count, src_design, att_design, obs_phase, obs_value, src_prior):
    at = lax.axis_index(TM)
    first = (at == 0).astype(jnp.int32).reshape(1)
    last = (at == lax.axis_size(TM) - 1).astype(jnp.int32).reshape(1)
    odd = (at % 2).astype(jnp.int32).reshape(1)
    place = lax.axis_index(SKY).astype(jnp.int32).reshape(1)
    line = lambda value: value.reshape(1, OBS_DEV)
    (state,) = call(open_kernel, "open", [STATE], work_ahead=1 << 32)
    work, sums, state = call(
        source_kernel,
        "source_sums",
        [WORK, ((160, 128), f32), STATE],
        obs_count, first, line(obs_source), src_design, line(obs_value), src_prior, state,
        aliases={6: 2},
        scalars=2,
    )
    parts = tm_parts(sums)
    (work,) = call(
        knot_kernel,
        "knot_spread",
        [WORK],
        obs_count, last, line(obs_knot), att_design, line(obs_phase), work,
        scalars=2,
        aliases={5: 0},
    )
    there = [KNOTS, EDGE, WORK, STATE]
    knots, edge, work, state = call(first_kernel, "first", there, *parts, work, state, aliases={4: 2, 5: 3})
    parts = sky_parts(knots, edge, odd)
    sums, work, state = call(
        start_kernel, "start", [((56, 128), f32), WORK, STATE], *parts, work, state, aliases={4: 1, 5: 2}
    )
    parts = tm_parts(sums)
    knots, edge, work, state = call(
        functools.partial(back_kernel, BEFORE), "back", there, *parts, work, state, aliases={4: 2, 5: 3}
    )
    parts = sky_parts(knots, edge, odd)
    sums, work, state = call(
        next_kernel, "next", [((64, 128), f32), WORK, STATE], *parts, work, state, aliases={4: 1, 5: 2}
    )
    parts = tm_parts(sums)
    knots, edge, work, state = call(
        functools.partial(back_kernel, AFTER), "back_again", there, *parts, work, state, aliases={4: 2, 5: 3}
    )
    parts = sky_parts(knots, edge, odd)
    return call(
        last_kernel,
        "last",
        [((4, 1, 256), f32), ((4, 1, 256), f32), ((5, 1024), f32)],
        place, *parts, state,
        scalars=1,
    )


def solution(mesh):
    torus = Mesh(mesh.devices.reshape(4, 4, 4, 2), SKY_TM)
    placed = (
        P(SKY_TM),
        P(SKY_TM),
        P(SKY_TM),
        P(None, SKY_TM),
        P(None, SKY_TM),
        P(SKY_TM),
        P(SKY_TM),
        P(None, SKY),
    )
    return jax.shard_map(
        shards,
        mesh=torus,
        in_specs=placed,
        out_specs=(P(None, TM, SKY), P(None, TM, SKY), P(None, SKY)),
        check_vma=False,
    )
```

```python
import functools

import jax
import jax.numpy as jnp
from jax import lax
from jax.experimental import pallas as pl
from jax.experimental.pallas import tpu as pltpu
from jax.sharding import Mesh
from jax.sharding import PartitionSpec as P

SKY = ("sky_0", "sky_1")
TM = ("tm_0", "tm_1")
SKY_TM = ("sky_0", "sky_1", "tm_0", "tm_1")

OBS_DEV = 4096
CHUNK = 1024
damping = 0.5
entry_pairs = [(row_at, col_at) for row_at in range(5) for col_at in range(row_at + 1)]


f32 = jnp.float32
bf16 = jnp.bfloat16


def split_rows(value):
    first = value.astype(bf16)
    rest = value - first.astype(f32)
    second = rest.astype(bf16)
    third = (rest - second.astype(f32)).astype(bf16)
    return jnp.concatenate([first, second, third], axis=0)


def join_rows(stacked):
    rows = stacked.shape[0] // 3
    return stacked[:rows] + (stacked[rows : 2 * rows] + stacked[2 * rows :])


def dot_nt(left, right):
    return lax.dot_general(left, right, (((1,), (1,)), ((), ())), preferred_element_type=f32)


def dot_nn(left, right):
    return lax.dot_general(left, right, (((1,), (0,)), ((), ())), preferred_element_type=f32)


def chunks():
    return [slice(start, start + CHUNK) for start in range(0, OBS_DEV, CHUNK)]


def four(refs):
    own, one, two, three = (ref[...] for ref in refs)
    return (own + two) + (one + three)


def lanes_from(start, rows):
    return lax.broadcasted_iota(jnp.int32, (rows, CHUNK), 1) + start


SOURCE_SPREAD = slice(0, 40)
KNOT_SPREAD = slice(40, 120)
IMAGE = slice(120, 121)
SOURCE_LANE = slice(121, 122)
KNOT_LANE = slice(122, 123)
START, MAPPED, RESIDUAL = (slice(at, at + 256) for at in (0, 256, 512))
FACTOR_A, FACTOR_B, BEFORE, AFTER, SCALAR = (slice(at, at + 128) for at in (768, 896, 1024, 1152, 1280))
WORK = ((128, OBS_DEV), f32)
STATE = ((80, 1408), f32)


def put(state, lanes, start, value):
    state[start : start + value.shape[0], lanes] = value


def get(state, lanes, start, rows):
    return state[start : start + rows, lanes]


GHOST_PLACES = ((SCALAR, 8), (SCALAR, 32), (SCALAR, 56), (BEFORE, 56))


def put_ghosts(state, ghosts):
    for at, (lanes, start) in enumerate(GHOST_PLACES):
        put(state, lanes, start, ghosts[:, 128 * at : 128 * at + 128])


def get_ghosts(state):
    return jnp.concatenate([get(state, lanes, start, 24) for lanes, start in GHOST_PLACES], axis=1)


def row_numbers(rows, lanes=CHUNK):
    return lax.broadcasted_iota(jnp.int32, (rows, lanes), 0).astype(f32).astype(bf16)


def hot_rows(numbers, lane_row):
    wanted = jnp.broadcast_to(lane_row, numbers.shape).astype(bf16)
    return jnp.where(numbers == wanted, jnp.ones_like(numbers), jnp.zeros_like(numbers))


def open_kernel(state):
    state[0:8, 0:128] = jnp.zeros((8, 128), f32)


def source_kernel(count_ref, first_ref, source_ref, g_ref, y_ref, prior_ref, _state, work, sums_ref, state):
    numbers = row_numbers(128)
    total = jnp.zeros((480, 128), f32)
    for at in chunks():
        live = lanes_from(at.start, 1) < count_ref[0]
        source = source_ref[:, at]
        lane = (source & 127).astype(f32)
        work[SOURCE_LANE, at] = lane
        mark = jnp.where(live, source >> 7, -1)
        chosen = jnp.where(lax.broadcasted_iota(jnp.int32, (8, CHUNK), 0) == mark, 1.0, 0.0)
        g = [g_ref[j : j + 1, at] for j in range(5)]
        y = y_ref[:, at]
        work[IMAGE, at] = y
        spread = [chosen * g[j] for j in range(5)]
        for j in range(5):
            work[8 * j : 8 * j + 8, at] = spread[j]
        rows = [spread[r] * g[c] for r, c in entry_pairs] + [spread[j] * y for j in range(5)]
        total = total + dot_nt(split_rows(jnp.concatenate(rows, axis=0)), hot_rows(numbers, lane))
    sums_ref[...] = join_rows(total)
    once = jnp.where(first_ref[0] == 1, 1.0, 0.0)
    for at, (row_at, col_at) in enumerate(entry_pairs):
        if row_at == col_at:
            prior = jnp.concatenate([prior_ref[row_at : row_at + 1, 128 * a : 128 * a + 128] for a in range(8)], axis=0)
            sums_ref[8 * at : 8 * at + 8] += prior * once


def knot_kernel(count_ref, last_ref, knot_ref, h_ref, phase_ref, _work, work):
    upper = lax.broadcasted_iota(jnp.int32, (8, CHUNK), 0) >> 2
    for at in chunks():
        live = lanes_from(at.start, 1) < count_ref[0]
        knot = knot_ref[:, at]
        high = knot >> 4
        work[KNOT_LANE, at] = high.astype(f32)
        h = jnp.where(live, h_ref[:, at], 0.0)
        h = jnp.concatenate([h, h], axis=0)
        phase = phase_ref[:, at]
        squared = phase * phase
        cubed = squared * phase
        rest = 1.0 - phase
        taps = (
            rest * rest * rest / 6.0,
            (3.0 * cubed - 6.0 * squared + 4.0) / 6.0,
            (-3.0 * cubed + 3.0 * squared + 3.0 * phase + 1.0) / 6.0,
            cubed / 6.0,
        )
        taps = [jnp.broadcast_to(tap, (8, CHUNK)) for tap in taps]
        ahead = upper - (knot & 15)
        kept = jnp.where((high == 255) & (last_ref[0] == 1), 0.0, 1.0)
        for q in range(10):
            gap = ahead + 2 * q
            weight = jnp.where(gap == 0, taps[0], 0.0)
            for m in range(1, 4):
                weight = jnp.where(gap == m, taps[m], weight)
            if q >= 8:
                weight = weight * kept
            row = KNOT_SPREAD.start + 8 * q
            work[row : row + 8, at] = weight * h


def ghost_kernel(count_ref, flat_ref, source_ref, g_ref, work, earlier_ref, later_ref):
    knot = flat_ref[...]
    order = lax.broadcasted_iota(jnp.int32, (32, 128), 0) * 128 + lax.broadcasted_iota(jnp.int32, (32, 128), 1)
    live = order < count_ref[0]
    across = jnp.where(
        lax.broadcasted_iota(jnp.int32, (128, 128), 0) < lax.broadcasted_iota(jnp.int32, (128, 128), 1), 1.0, 0.0
    ).astype(bf16)
    down = jnp.where(
        lax.broadcasted_iota(jnp.int32, (32, 32), 0) > lax.broadcasted_iota(jnp.int32, (32, 32), 1), 1.0, 0.0
    ).astype(bf16)
    numbers = row_numbers(256, 128)
    for chosen, spread_at, ref in ((live & (knot >= 4093), 104, later_ref), (live & (knot < 3), 40, earlier_ref)):
        mark = jnp.where(chosen, 1.0, 0.0).astype(bf16)
        rank = dot_nn(mark, across) + jnp.sum(dot_nn(down, mark), axis=1, keepdims=True)
        rank = jnp.where(chosen, rank, -1.0)
        total = jnp.zeros((72, 256), f32)
        for at in chunks():
            first = at.start // 128
            slots = jnp.concatenate([hot_rows(numbers, rank[row : row + 1]) for row in range(first, first + CHUNK // 128)], axis=1)
            data = jnp.concatenate(
                [work[spread_at : spread_at + 16, at], g_ref[:, at], source_ref[:, at].astype(f32), work[IMAGE, at], jnp.zeros((1, CHUNK), f32)],
                axis=0,
            )
            total = total + dot_nt(split_rows(data), slots)
        ref[...] = join_rows(total)


def ghost_sums(solved, ghosts, values):
    source = ghosts[21:22].astype(jnp.int32)
    picked = join_rows(dot_nn(solved, hot_rows(row_numbers(128, 512), (source & 127).astype(f32))))
    fitted = functools.reduce(jnp.add, [tile(picked, j) * ghosts[16 + j : 17 + j] for j in range(5)])
    fitted = jnp.where(lax.broadcasted_iota(jnp.int32, (8, 512), 0) == (source >> 7), fitted, 0.0)
    weighted = ghosts[0:16] * (values - jnp.sum(fitted, axis=0, keepdims=True))
    return jnp.sum(weighted[:, 0:256], axis=1, keepdims=True), jnp.sum(weighted[:, 256:512], axis=1, keepdims=True)


def end_tile(at_tm, high, low):
    lane = lax.broadcasted_iota(jnp.int32, (8, 128), 1)
    result = jnp.zeros((8, 128), f32)
    for place, part in enumerate((high[0:8], high[8:16], low[0:8], low[8:16])):
        result = jnp.where(lane == at_tm + 16 * place, part, result)
    return result


def end_parts(at_tm, ends):
    lane = lax.broadcasted_iota(jnp.int32, (8, 128), 1)
    pick = lambda at: jnp.sum(jnp.where(lane == at, ends, 0.0), axis=1, keepdims=True)
    earlier = jnp.concatenate([pick(at_tm - 1), pick(at_tm + 15)], axis=0)
    later = jnp.concatenate([pick(at_tm + 33), pick(at_tm + 49)], axis=0)
    return earlier, later


def tile(value, at):
    return value[8 * at : 8 * at + 8]


def factor_of(value):
    return {pair: tile(value, at) for at, pair in enumerate(entry_pairs)}


def factorize(normal):
    factor = {}
    for row_at in range(5):
        for col_at in range(row_at + 1):
            running = normal[row_at, col_at]
            for inner_at in range(col_at):
                running = running - factor[row_at, inner_at] * factor[col_at, inner_at]
            if row_at == col_at:
                factor[row_at, row_at] = 1.0 / jnp.sqrt(running)
            else:
                factor[row_at, col_at] = running * factor[col_at, col_at]
    return factor


def chol_solve(factor, target):
    forward = []
    for row_at in range(5):
        running = target[row_at]
        for inner_at in range(row_at):
            running = running - factor[row_at, inner_at] * forward[inner_at]
        forward.append(running * factor[row_at, row_at])
    result = [None] * 5
    for row_at in reversed(range(5)):
        running = forward[row_at]
        for inner_at in range(row_at + 1, 5):
            running = running - factor[inner_at, row_at] * result[inner_at]
        result[row_at] = running * factor[row_at, row_at]
    return result


def eliminate_and_spread(solved, work):
    source_numbers, knot_numbers = row_numbers(128), row_numbers(256)
    total = jnp.zeros((240, 256), f32)
    for at in chunks():
        picked = join_rows(dot_nn(solved, hot_rows(source_numbers, work[SOURCE_LANE, at])))
        fitted = jnp.sum(picked * work[SOURCE_SPREAD, at], axis=0, keepdims=True)
        cleaned = work[IMAGE, at] - fitted
        total = total + dot_nt(split_rows(work[KNOT_SPREAD, at] * cleaned), hot_rows(knot_numbers, work[KNOT_LANE, at]))
    return join_rows(total)


def with_ends(total, earlier, later, energy):
    lane = lax.broadcasted_iota(jnp.int32, (16, 256), 1)
    within = lax.broadcasted_iota(jnp.int32, (16, 256), 0) < 12
    low = total[0:16] + jnp.where(within & (lane == 0), earlier, 0.0)
    high = total[64:80] + jnp.where(within & (lane == 255), later, 0.0)
    if energy is not None:
        high = jnp.concatenate([high[0:12], jnp.concatenate([energy[0:4], energy[4:8]], axis=1)], axis=0)
    return jnp.concatenate([low, total[16:64], high], axis=0)


def first_kernel(own, one, two, three, earlier_ref, later_ref, _work, _state, knots_ref, work, state):
    sums = four((own, one, two, three))
    factor = factorize(factor_of(sums))
    stacked = jnp.concatenate([factor[pair] for pair in entry_pairs], axis=0)
    put(state, FACTOR_A, 0, stacked[0:80])
    put(state, FACTOR_B, 0, stacked[80:120])
    put(state, FACTOR_B, 40, sums[120:160])
    ghosts = jnp.concatenate([earlier_ref[...], later_ref[...]], axis=1)
    put_ghosts(state, ghosts)
    solved = split_rows(jnp.concatenate(chol_solve(factor, [tile(sums, 15 + j) for j in range(5)]), axis=0))
    earlier, later = ghost_sums(solved, ghosts, ghosts[22:23])
    knots_ref[...] = with_ends(eliminate_and_spread(solved, work), earlier, later, None)


def kept_factor(state):
    return factor_of(jnp.concatenate([get(state, FACTOR_A, 0, 80), get(state, FACTOR_B, 0, 40)], axis=0))


def back(lanes, at_tm, parts, work, state):
    sums = four(parts)
    put(state, lanes, 0, sums[:-8])
    target = [tile(sums, j) for j in range(5)]
    solved = chol_solve(kept_factor(state), target)
    energy = tile(sums, 5)
    for j in range(5):
        energy = energy - target[j] * solved[j]
    solved = split_rows(jnp.concatenate(solved, axis=0))
    ends = zip(ghost_sums(solved, get_ghosts(state), 0.0), end_parts(at_tm, sums[-8:]))
    earlier, later = (ghost + image for ghost, image in ends)
    return with_ends(eliminate_and_spread(solved, work), earlier, later, energy), energy


def back_kernel(tm_ref, own, one, two, three, _work, _state, knots_ref, work, state):
    knots_ref[...], _ = back(BEFORE, tm_ref[0], (own, one, two, three), work, state)


def back_to_owners_kernel(tm_ref, own, one, two, three, _work, _state, blocks_ref, work, state):
    knots, energy = back(AFTER, tm_ref[0], (own, one, two, three), work, state)
    knots = assembled(knots)
    place = lax.broadcasted_iota(jnp.int32, (8, 128), 1) >> 4
    for owner in range(16):
        half = slice(128 * (owner // 8), 128 * (owner // 8) + 128)
        block = jnp.zeros((8, 128), f32)
        for q in range(8):
            block = jnp.where(place == q, moved(knots[8 * q : 8 * q + 8, half], (16 * (q - owner)) % 128), block)
        blocks_ref[owner, 0:8] = block
        blocks_ref[owner, 8:16] = energy


def moved(value, lanes):
    return value if isinstance(lanes, int) and lanes == 0 else pltpu.roll(value, lanes, 1)


def assembled(knots):
    lane = lax.broadcasted_iota(jnp.int32, (16, 256), 1)
    row = lax.broadcasted_iota(jnp.int32, (16, 256), 0)
    beyond = jnp.where(row < 12, knots[64:80], 0.0)
    low = knots[0:16] + jnp.where(lane == 0, 0.0, pltpu.roll(beyond, 1, 1))
    high = jnp.where(row < 12, jnp.where(lane == 255, beyond, pltpu.roll(low, 255, 1)), 0.0)
    return jnp.concatenate([low, knots[16:64], high], axis=0)


def energy_of(knots):
    return jnp.sum(knots[76:80])


def folded(left, right):
    product = left[0:64] * right[0:64]
    product = product[:, 0:128] + product[:, 128:256]
    return functools.reduce(jnp.add, [tile(product, at) for at in range(8)])


def lane_blocks(value):
    return functools.reduce(jnp.add, [value[:, start : start + 128] for start in range(0, CHUNK, 128)])


def gather_and_sum(at_tm, field, work):
    source_numbers, knot_numbers = row_numbers(128), row_numbers(256)
    parts = split_rows(field)
    total = jnp.zeros((120, 128), f32)
    square = jnp.zeros((1, 128), f32)
    high = jnp.zeros((16, 128), f32)
    low = jnp.zeros((16, 128), f32)
    for at in chunks():
        knot_lane = work[KNOT_LANE, at]
        picked = join_rows(dot_nn(parts, hot_rows(knot_numbers, knot_lane)))
        image = jnp.sum(picked * work[KNOT_SPREAD, at], axis=0, keepdims=True)
        work[IMAGE, at] = image
        square = square + lane_blocks(image * image)
        high = high + lane_blocks(work[104:120, at] * jnp.where(knot_lane == 255.0, image, 0.0))
        low = low + lane_blocks(work[40:56, at] * jnp.where(knot_lane == 0.0, image, 0.0))
        total = total + dot_nt(split_rows(work[SOURCE_SPREAD, at] * image), hot_rows(source_numbers, work[SOURCE_LANE, at]))
    ends = end_tile(at_tm, jnp.sum(high, axis=1, keepdims=True), jnp.sum(low, axis=1, keepdims=True))
    return join_rows(total), jnp.concatenate([square, jnp.zeros((7, 128), f32)], axis=0), ends


def start_kernel(tm_ref, own, one, two, three, _work, _state, sums_ref, work, state):
    residual = assembled(four((own, one, two, three)))
    put(state, START, 0, residual)
    sums, square, ends = gather_and_sum(tm_ref[0], residual, work)
    sums_ref[...] = jnp.concatenate([sums, square, folded(residual, residual), ends], axis=0)


def next_kernel(tm_ref, own, one, two, three, _work, _state, sums_ref, work, state):
    knots = four((own, one, two, three))
    direction = get(state, START, 0, 80)
    mapped = assembled(knots) + damping * direction
    norm_now = jnp.sum(get(state, BEFORE, 48, 8))
    product = energy_of(knots) + damping * norm_now
    residual = direction - (norm_now / product) * mapped
    put(state, MAPPED, 0, mapped)
    put(state, RESIDUAL, 0, residual)
    put(state, SCALAR, 0, jnp.zeros((8, 128), f32) + product)
    sums, square, ends = gather_and_sum(tm_ref[0], residual, work)
    sums_ref[...] = jnp.concatenate([sums, square, folded(residual, residual), folded(residual, mapped), ends], axis=0)


def last_kernel(place_ref, blocks_ref, state, solution_ref, left_ref, source_ref):
    place = place_ref[0]
    blocks = functools.reduce(jnp.add, [blocks_ref[at] for at in range(16)])
    lane_place = lax.broadcasted_iota(jnp.int32, (8, 128), 1) >> 4

    def own_lanes(lanes):
        result = jnp.zeros((8, 128), f32)
        for q in range(8):
            rows = get(state, lanes, 8 * q, 8)
            rows = jnp.where(place >= 8, rows[:, 128:256], rows[:, 0:128])
            rows = pltpu.roll(rows, (16 * (q - place)) & 127, 1)
            result = jnp.where(lane_place == q, rows, result)
        return result

    start, mapped, residual = own_lanes(START), own_lanes(MAPPED), own_lanes(RESIDUAL)
    image = blocks[0:8] + damping * residual
    before, after = get(state, BEFORE, 0, 56), get(state, AFTER, 0, 64)
    norm_first = jnp.sum(before[48:56])
    product_first = jnp.max(get(state, SCALAR, 0, 8))
    alpha_first = norm_first / product_first
    norm_now = jnp.sum(after[48:56])
    crossed = jnp.sum(after[56:64])
    beta = norm_now / norm_first
    product = jnp.sum(blocks[8:16]) + damping * norm_now + beta * (2.0 * crossed + beta * product_first)
    alpha = norm_now / product
    from_start = alpha_first + alpha * beta
    solution = from_start * start + alpha * residual
    left = residual - alpha * (image + beta * mapped)
    both = split_rows(jnp.concatenate([solution, left], axis=0))
    held = lax.broadcasted_iota(jnp.int32, (128, 256), 0)
    wanted = lax.broadcasted_iota(jnp.int32, (128, 256), 1)
    same = (held & 15) == (wanted >> 4)
    halves = [
        join_rows(dot_nn(both, jnp.where(same & ((wanted & 15) == 2 * (held >> 4) + upper), 1.0, 0.0).astype(bf16)))
        for upper in range(2)
    ]
    for at, ref in enumerate((solution_ref, left_ref)):
        own_rows = halves[0][8 * at : 8 * at + 4] + halves[1][8 * at + 4 : 8 * at + 8]
        for c in range(4):
            ref[c] = own_rows[c : c + 1]
    rhs = get(state, FACTOR_B, 40, 40)
    target = [tile(rhs, j) - from_start * tile(before, j) - alpha * tile(after, j) for j in range(5)]
    solved = chol_solve(kept_factor(state), target)
    for j in range(5):
        for a in range(8):
            source_ref[j : j + 1, 128 * a : 128 * a + 128] = solved[j][a : a + 1]


VMEM = pl.BlockSpec(memory_space=pltpu.VMEM)
SMEM = pl.BlockSpec(memory_space=pltpu.SMEM)


def call(kernel, name, outs, *operands, scalars=0, aliases=None, work_ahead=0):
    specs = [SMEM] * scalars + [VMEM] * (len(operands) - scalars)
    shapes = [jax.ShapeDtypeStruct(shape, dtype) for shape, dtype in outs]
    return pl.pallas_call(
        kernel,
        out_shape=shapes,
        in_specs=specs,
        out_specs=[VMEM] * len(outs),
        input_output_aliases=aliases or {},
        compiler_params=pltpu.CompilerParams(vmem_limit_bytes=8 * 1024 * 1024),
        cost_estimate=pl.CostEstimate(flops=work_ahead, bytes_accessed=0, transcendentals=0) if work_ahead else None,
        name=name,
    )(*operands)


def ring_parts(value, axis):
    count = lax.axis_size(axis)
    return [value] + [
        lax.ppermute(value, axis, [(at, (at + step) % count) for at in range(count)]) for step in (1, 2, 3)
    ]


def shifted(value, step):
    count = lax.axis_size(TM)
    return lax.ppermute(value, TM, [(at, at + step) for at in range(count) if 0 <= at + step < count])


def tm_parts(value):
    value = value + lax.ppermute(value, "tm_1", [(0, 1), (1, 0)])
    return ring_parts(value, "tm_0")


def sky_parts(knots):
    own, one, two, three = ring_parts(knots, "sky_1")
    return ring_parts((own + two) + (one + three), "sky_0")


KNOTS = ((80, 256), f32)
GHOSTS = ((24, 256), f32)


def shards(obs_source, obs_knot, obs_count, src_design, att_design, obs_phase, obs_value, src_prior):
    at = lax.axis_index(TM)
    first = (at == 0).astype(jnp.int32).reshape(1)
    last = (at == lax.axis_size(TM) - 1).astype(jnp.int32).reshape(1)
    tm = at.astype(jnp.int32).reshape(1)
    place = lax.axis_index(SKY).astype(jnp.int32).reshape(1)
    line = lambda value: value.reshape(1, OBS_DEV)
    (state,) = call(open_kernel, "open", [STATE], work_ahead=1 << 32)
    work, sums, state = call(
        source_kernel,
        "source_sums",
        [WORK, ((160, 128), f32), STATE],
        obs_count, first, line(obs_source), src_design, line(obs_value), src_prior, state,
        aliases={6: 2},
        scalars=2,
    )
    parts = tm_parts(sums)
    (work,) = call(
        knot_kernel,
        "knot_spread",
        [WORK],
        obs_count, last, line(obs_knot), att_design, line(obs_phase), work,
        scalars=2,
        aliases={5: 0},
    )
    earlier, later = call(
        ghost_kernel,
        "ghosts",
        [GHOSTS, GHOSTS],
        obs_count, obs_knot.reshape(32, 128), line(obs_source), src_design, work,
        scalars=1,
    )
    ends = (shifted(later, 1), shifted(earlier, -1))
    knots, work, state = call(
        first_kernel, "first", [KNOTS, WORK, STATE], *parts, *ends, work, state, aliases={6: 1, 7: 2}
    )
    parts = sky_parts(knots)
    kept = dict(scalars=1, aliases={5: 1, 6: 2})
    sums, work, state = call(start_kernel, "start", [((64, 128), f32), WORK, STATE], tm, *parts, work, state, **kept)
    parts = tm_parts(sums)
    knots, work, state = call(back_kernel, "back", [KNOTS, WORK, STATE], tm, *parts, work, state, **kept)
    parts = sky_parts(knots)
    sums, work, state = call(next_kernel, "next", [((72, 128), f32), WORK, STATE], tm, *parts, work, state, **kept)
    parts = tm_parts(sums)
    blocks, work, state = call(
        back_to_owners_kernel, "back_to_owners", [((16, 16, 128), f32), WORK, STATE], tm, *parts, work, state, **kept
    )
    blocks = lax.all_to_all(blocks, SKY, 0, 0, tiled=True)
    return call(
        last_kernel,
        "last",
        [((4, 1, 256), f32), ((4, 1, 256), f32), ((5, 1024), f32)],
        place, blocks, state,
        scalars=1,
    )


def solution(mesh):
    torus = Mesh(mesh.devices.reshape(4, 4, 4, 2), SKY_TM)
    placed = (
        P(SKY_TM),
        P(SKY_TM),
        P(SKY_TM),
        P(None, SKY_TM),
        P(None, SKY_TM),
        P(SKY_TM),
        P(SKY_TM),
        P(None, SKY),
    )
    return jax.shard_map(
        shards,
        mesh=torus,
        in_specs=placed,
        out_specs=(P(None, TM, SKY), P(None, TM, SKY), P(None, SKY)),
        check_vma=False,
    )
```

```python
import functools

import jax
import jax.numpy as jnp
from jax import lax
from jax.experimental import pallas as pl
from jax.experimental.pallas import tpu as pltpu
from jax.sharding import Mesh
from jax.sharding import PartitionSpec as P

SKY = ("sky_0", "sky_1")
TM = ("tm_0", "tm_1")
SKY_TM = ("sky_0", "sky_1", "tm_0", "tm_1")

OBS_DEV = 4096
CHUNK = 4096
damping = 0.5
entry_pairs = [(row_at, col_at) for row_at in range(5) for col_at in range(row_at + 1)]


f32 = jnp.float32
bf16 = jnp.bfloat16


def split_rows(value):
    first = value.astype(bf16)
    rest = value - first.astype(f32)
    second = rest.astype(bf16)
    third = (rest - second.astype(f32)).astype(bf16)
    return jnp.concatenate([first, second, third], axis=0)


def join_rows(stacked):
    rows = stacked.shape[0] // 3
    return stacked[:rows] + (stacked[rows : 2 * rows] + stacked[2 * rows :])


def dot_nt(left, right):
    return lax.dot_general(left, right, (((1,), (1,)), ((), ())), preferred_element_type=f32)


def dot_nn(left, right):
    return lax.dot_general(left, right, (((1,), (0,)), ((), ())), preferred_element_type=f32)


def chunks():
    return [slice(start, start + CHUNK) for start in range(0, OBS_DEV, CHUNK)]


def four(refs):
    own, one, two, three = (ref[...] for ref in refs)
    return (own + two) + (one + three)


def lanes_from(start, rows):
    return lax.broadcasted_iota(jnp.int32, (rows, CHUNK), 1) + start


SOURCE_SPREAD = slice(0, 40)
KNOT_SPREAD = slice(40, 120)
IMAGE = slice(120, 121)
SOURCE_LANE = slice(121, 122)
KNOT_LANE = slice(122, 123)
START, MAPPED, RESIDUAL = (slice(at, at + 256) for at in (0, 256, 512))
FACTOR_A, FACTOR_B, BEFORE, AFTER, SCALAR = (slice(at, at + 128) for at in (768, 896, 1024, 1152, 1280))
WORK = ((128, OBS_DEV), f32)
STATE = ((80, 1408), f32)


def put(state, lanes, start, value):
    state[start : start + value.shape[0], lanes] = value


def get(state, lanes, start, rows):
    return state[start : start + rows, lanes]


GHOST_PLACES = ((SCALAR, 8), (SCALAR, 32), (SCALAR, 56), (BEFORE, 56))


def put_ghosts(state, ghosts):
    for at, (lanes, start) in enumerate(GHOST_PLACES):
        put(state, lanes, start, ghosts[:, 128 * at : 128 * at + 128])


def get_ghosts(state):
    return jnp.concatenate([get(state, lanes, start, 24) for lanes, start in GHOST_PLACES], axis=1)


def row_numbers(rows, lanes=CHUNK):
    return lax.broadcasted_iota(jnp.int32, (rows, lanes), 0).astype(f32).astype(bf16)


def hot_rows(numbers, lane_row):
    wanted = jnp.broadcast_to(lane_row, numbers.shape).astype(bf16)
    return jnp.where(numbers == wanted, jnp.ones_like(numbers), jnp.zeros_like(numbers))


def open_kernel(state):
    state[0:8, 0:128] = jnp.zeros((8, 128), f32)


def source_kernel(count_ref, first_ref, source_ref, g_ref, y_ref, prior_ref, _state, work, sums_ref, state):
    numbers = row_numbers(128)
    total = jnp.zeros((480, 128), f32)
    for at in chunks():
        live = lanes_from(at.start, 1) < count_ref[0]
        source = source_ref[:, at]
        lane = (source & 127).astype(f32)
        work[SOURCE_LANE, at] = lane
        mark = jnp.where(live, source >> 7, -1)
        chosen = jnp.where(lax.broadcasted_iota(jnp.int32, (8, CHUNK), 0) == mark, 1.0, 0.0)
        g = [g_ref[j : j + 1, at] for j in range(5)]
        y = y_ref[:, at]
        work[IMAGE, at] = y
        spread = [chosen * g[j] for j in range(5)]
        for j in range(5):
            work[8 * j : 8 * j + 8, at] = spread[j]
        rows = [spread[r] * g[c] for r, c in entry_pairs] + [spread[j] * y for j in range(5)]
        total = total + dot_nt(split_rows(jnp.concatenate(rows, axis=0)), hot_rows(numbers, lane))
    sums_ref[...] = join_rows(total)
    once = jnp.where(first_ref[0] == 1, 1.0, 0.0)
    for at, (row_at, col_at) in enumerate(entry_pairs):
        if row_at == col_at:
            prior = jnp.concatenate([prior_ref[row_at : row_at + 1, 128 * a : 128 * a + 128] for a in range(8)], axis=0)
            sums_ref[8 * at : 8 * at + 8] += prior * once


def knot_kernel(count_ref, last_ref, knot_ref, h_ref, phase_ref, _work, work):
    upper = lax.broadcasted_iota(jnp.int32, (8, CHUNK), 0) >> 2
    for at in chunks():
        live = lanes_from(at.start, 1) < count_ref[0]
        knot = knot_ref[:, at]
        high = knot >> 4
        work[KNOT_LANE, at] = high.astype(f32)
        h = jnp.where(live, h_ref[:, at], 0.0)
        h = jnp.concatenate([h, h], axis=0)
        phase = phase_ref[:, at]
        squared = phase * phase
        cubed = squared * phase
        rest = 1.0 - phase
        taps = (
            rest * rest * rest / 6.0,
            (3.0 * cubed - 6.0 * squared + 4.0) / 6.0,
            (-3.0 * cubed + 3.0 * squared + 3.0 * phase + 1.0) / 6.0,
            cubed / 6.0,
        )
        taps = [jnp.broadcast_to(tap, (8, CHUNK)) for tap in taps]
        ahead = upper - (knot & 15)
        kept = jnp.where((high == 255) & (last_ref[0] == 1), 0.0, 1.0)
        for q in range(10):
            gap = ahead + 2 * q
            weight = jnp.where(gap == 0, taps[0], 0.0)
            for m in range(1, 4):
                weight = jnp.where(gap == m, taps[m], weight)
            if q >= 8:
                weight = weight * kept
            row = KNOT_SPREAD.start + 8 * q
            work[row : row + 8, at] = weight * h


def ghost_kernel(count_ref, tm_ref, flat_ref, source_ref, g_ref, work, earlier_ref, later_ref, twin_ref):
    knot = flat_ref[...]
    order = lax.broadcasted_iota(jnp.int32, (32, 128), 0) * 128 + lax.broadcasted_iota(jnp.int32, (32, 128), 1)
    live = order < count_ref[0]
    across = jnp.where(
        lax.broadcasted_iota(jnp.int32, (128, 128), 0) < lax.broadcasted_iota(jnp.int32, (128, 128), 1), 1.0, 0.0
    ).astype(bf16)
    down = jnp.where(
        lax.broadcasted_iota(jnp.int32, (32, 32), 0) > lax.broadcasted_iota(jnp.int32, (32, 32), 1), 1.0, 0.0
    ).astype(bf16)
    numbers = row_numbers(256, 128)
    at_low = live & (knot < 3) & (tm_ref[0] > 0)
    for chosen, spread_at, ref in ((live & (knot >= 4093), 104, later_ref), (at_low, 40, earlier_ref)):
        mark = jnp.where(chosen, 1.0, 0.0).astype(bf16)
        rank = dot_nn(mark, across) + jnp.sum(dot_nn(down, mark), axis=1, keepdims=True)
        rank = jnp.where(chosen, rank, -1.0)
        total = jnp.zeros((72, 256), f32)
        for at in chunks():
            first = at.start // 128
            slots = jnp.concatenate([hot_rows(numbers, rank[row : row + 1]) for row in range(first, first + CHUNK // 128)], axis=1)
            data = jnp.concatenate(
                [work[spread_at : spread_at + 16, at], g_ref[:, at], source_ref[:, at].astype(f32), work[IMAGE, at], jnp.zeros((1, CHUNK), f32)],
                axis=0,
            )
            total = total + dot_nt(split_rows(data), slots)
        total = join_rows(total)
        ref[0:24] = total[:, 0:128]
        ref[24:48] = total[:, 128:256]
    twin_ref[...] = jnp.where((tm_ref[0] & 1) == 1, earlier_ref[...], later_ref[...])


def ghost_sums(solved, ghosts, values):
    source = ghosts[21:22].astype(jnp.int32)
    picked = join_rows(dot_nn(solved, hot_rows(row_numbers(128, 512), (source & 127).astype(f32))))
    fitted = functools.reduce(jnp.add, [tile(picked, j) * ghosts[16 + j : 17 + j] for j in range(5)])
    fitted = jnp.where(lax.broadcasted_iota(jnp.int32, (8, 512), 0) == (source >> 7), fitted, 0.0)
    weighted = ghosts[0:16] * (values - jnp.sum(fitted, axis=0, keepdims=True))
    return jnp.sum(weighted[:, 0:256], axis=1, keepdims=True), jnp.sum(weighted[:, 256:512], axis=1, keepdims=True)


def end_tile(at_tm, high, low):
    lane = lax.broadcasted_iota(jnp.int32, (8, 128), 1)
    result = jnp.zeros((8, 128), f32)
    for place, part in enumerate((high[0:8], high[8:16], low[0:8], low[8:16])):
        result = jnp.where(lane == at_tm + 16 * place, part, result)
    return result


def end_parts(at_tm, ends):
    lane = lax.broadcasted_iota(jnp.int32, (8, 128), 1)
    pick = lambda at: jnp.sum(jnp.where(lane == at, ends, 0.0), axis=1, keepdims=True)
    earlier = jnp.concatenate([pick(at_tm - 1), pick(at_tm + 15)], axis=0)
    later = jnp.concatenate([pick(at_tm + 33), pick(at_tm + 49)], axis=0)
    return earlier, later


def tile(value, at):
    return value[8 * at : 8 * at + 8]


def factor_of(value):
    return {pair: tile(value, at) for at, pair in enumerate(entry_pairs)}


def factorize(normal):
    factor = {}
    for row_at in range(5):
        for col_at in range(row_at + 1):
            running = normal[row_at, col_at]
            for inner_at in range(col_at):
                running = running - factor[row_at, inner_at] * factor[col_at, inner_at]
            if row_at == col_at:
                factor[row_at, row_at] = 1.0 / jnp.sqrt(running)
            else:
                factor[row_at, col_at] = running * factor[col_at, col_at]
    return factor


def chol_solve(factor, target):
    forward = []
    for row_at in range(5):
        running = target[row_at]
        for inner_at in range(row_at):
            running = running - factor[row_at, inner_at] * forward[inner_at]
        forward.append(running * factor[row_at, row_at])
    result = [None] * 5
    for row_at in reversed(range(5)):
        running = forward[row_at]
        for inner_at in range(row_at + 1, 5):
            running = running - factor[inner_at, row_at] * result[inner_at]
        result[row_at] = running * factor[row_at, row_at]
    return result


def eliminate_and_spread(solved, work):
    source_numbers, knot_numbers = row_numbers(128), row_numbers(256)
    total = jnp.zeros((240, 256), f32)
    for at in chunks():
        picked = join_rows(dot_nn(solved, hot_rows(source_numbers, work[SOURCE_LANE, at])))
        fitted = jnp.sum(picked * work[SOURCE_SPREAD, at], axis=0, keepdims=True)
        cleaned = work[IMAGE, at] - fitted
        total = total + dot_nt(split_rows(work[KNOT_SPREAD, at] * cleaned), hot_rows(knot_numbers, work[KNOT_LANE, at]))
    return join_rows(total)


def with_ends(total, earlier, later, energy):
    lane = lax.broadcasted_iota(jnp.int32, (16, 256), 1)
    within = lax.broadcasted_iota(jnp.int32, (16, 256), 0) < 12
    low = total[0:16] + jnp.where(within & (lane == 0), earlier, 0.0)
    high = total[64:80] + jnp.where(within & (lane == 255), later, 0.0)
    if energy is not None:
        high = jnp.concatenate([high[0:12], jnp.concatenate([energy[0:4], energy[4:8]], axis=1)], axis=0)
    return jnp.concatenate([low, total[16:64], high], axis=0)


def first_kernel(tm_ref, own, one, two, three, twin, _work, _state, knots_ref, work, state):
    sums = (own[0:160] + two[...]) + (one[0:160] + three[0:160])
    odd = (tm_ref[0] & 1) == 1
    earlier = jnp.where(odd, twin[...], one[160:208])
    later = jnp.where(odd, three[160:208], twin[...])
    factor = factorize(factor_of(sums))
    stacked = jnp.concatenate([factor[pair] for pair in entry_pairs], axis=0)
    put(state, FACTOR_A, 0, stacked[0:80])
    put(state, FACTOR_B, 0, stacked[80:120])
    put(state, FACTOR_B, 40, sums[120:160])
    ghosts = jnp.concatenate([earlier[0:24], earlier[24:48], later[0:24], later[24:48]], axis=1)
    put_ghosts(state, ghosts)
    solved = split_rows(jnp.concatenate(chol_solve(factor, [tile(sums, 15 + j) for j in range(5)]), axis=0))
    earlier, later = ghost_sums(solved, ghosts, ghosts[22:23])
    knots_ref[...] = with_ends(eliminate_and_spread(solved, work), earlier, later, None)


def kept_factor(state):
    return factor_of(jnp.concatenate([get(state, FACTOR_A, 0, 80), get(state, FACTOR_B, 0, 40)], axis=0))


def back(lanes, at_tm, parts, work, state):
    sums = four(parts)
    put(state, lanes, 0, sums[:-8])
    target = [tile(sums, j) for j in range(5)]
    solved = chol_solve(kept_factor(state), target)
    energy = tile(sums, 5)
    for j in range(5):
        energy = energy - target[j] * solved[j]
    solved = split_rows(jnp.concatenate(solved, axis=0))
    ends = zip(ghost_sums(solved, get_ghosts(state), 0.0), end_parts(at_tm, sums[-8:]))
    earlier, later = (ghost + image for ghost, image in ends)
    return with_ends(eliminate_and_spread(solved, work), earlier, later, energy), energy


def back_kernel(tm_ref, own, one, two, three, _work, _state, knots_ref, work, state):
    knots_ref[...], _ = back(BEFORE, tm_ref[0], (own, one, two, three), work, state)


def back_to_owners_kernel(tm_ref, own, one, two, three, _work, _state, blocks_ref, work, state):
    knots, energy = back(AFTER, tm_ref[0], (own, one, two, three), work, state)
    knots = assembled(knots)
    place = lax.broadcasted_iota(jnp.int32, (8, 128), 1) >> 4
    for owner in range(16):
        half = slice(128 * (owner // 8), 128 * (owner // 8) + 128)
        block = jnp.zeros((8, 128), f32)
        for q in range(8):
            block = jnp.where(place == q, moved(knots[8 * q : 8 * q + 8, half], (16 * (q - owner)) % 128), block)
        blocks_ref[owner, 0:8] = block
        blocks_ref[owner, 8:16] = energy


def moved(value, lanes):
    return value if isinstance(lanes, int) and lanes == 0 else pltpu.roll(value, lanes, 1)


def assembled(knots):
    lane = lax.broadcasted_iota(jnp.int32, (16, 256), 1)
    row = lax.broadcasted_iota(jnp.int32, (16, 256), 0)
    beyond = jnp.where(row < 12, knots[64:80], 0.0)
    low = knots[0:16] + jnp.where(lane == 0, 0.0, pltpu.roll(beyond, 1, 1))
    high = jnp.where(row < 12, jnp.where(lane == 255, beyond, pltpu.roll(low, 255, 1)), 0.0)
    return jnp.concatenate([low, knots[16:64], high], axis=0)


def energy_of(knots):
    return jnp.sum(knots[76:80])


def folded(left, right):
    product = left[0:64] * right[0:64]
    product = product[:, 0:128] + product[:, 128:256]
    return functools.reduce(jnp.add, [tile(product, at) for at in range(8)])


def lane_blocks(value):
    return functools.reduce(jnp.add, [value[:, start : start + 128] for start in range(0, CHUNK, 128)])


def gather_and_sum(at_tm, field, work):
    source_numbers, knot_numbers = row_numbers(128), row_numbers(256)
    parts = split_rows(field)
    total = jnp.zeros((120, 128), f32)
    square = jnp.zeros((1, 128), f32)
    high = jnp.zeros((16, 128), f32)
    low = jnp.zeros((16, 128), f32)
    for at in chunks():
        knot_lane = work[KNOT_LANE, at]
        picked = join_rows(dot_nn(parts, hot_rows(knot_numbers, knot_lane)))
        image = jnp.sum(picked * work[KNOT_SPREAD, at], axis=0, keepdims=True)
        work[IMAGE, at] = image
        square = square + lane_blocks(image * image)
        high = high + lane_blocks(work[104:120, at] * jnp.where(knot_lane == 255.0, image, 0.0))
        low = low + lane_blocks(work[40:56, at] * jnp.where(knot_lane == 0.0, image, 0.0))
        total = total + dot_nt(split_rows(work[SOURCE_SPREAD, at] * image), hot_rows(source_numbers, work[SOURCE_LANE, at]))
    ends = end_tile(at_tm, jnp.sum(high, axis=1, keepdims=True), jnp.sum(low, axis=1, keepdims=True))
    return join_rows(total), jnp.concatenate([square, jnp.zeros((7, 128), f32)], axis=0), ends


def start_kernel(tm_ref, own, one, two, three, _work, _state, sums_ref, work, state):
    residual = assembled(four((own, one, two, three)))
    put(state, START, 0, residual)
    sums, square, ends = gather_and_sum(tm_ref[0], residual, work)
    sums_ref[...] = jnp.concatenate([sums, square, folded(residual, residual), ends], axis=0)


def next_kernel(tm_ref, own, one, two, three, _work, _state, sums_ref, work, state):
    knots = four((own, one, two, three))
    direction = get(state, START, 0, 80)
    mapped = assembled(knots) + damping * direction
    norm_now = jnp.sum(get(state, BEFORE, 48, 8))
    product = energy_of(knots) + damping * norm_now
    residual = direction - (norm_now / product) * mapped
    put(state, MAPPED, 0, mapped)
    put(state, RESIDUAL, 0, residual)
    put(state, SCALAR, 0, jnp.zeros((8, 128), f32) + product)
    sums, square, ends = gather_and_sum(tm_ref[0], residual, work)
    sums_ref[...] = jnp.concatenate([sums, square, folded(residual, residual), folded(residual, mapped), ends], axis=0)


def last_kernel(place_ref, blocks_ref, state, solution_ref, left_ref, source_ref):
    place = place_ref[0]
    blocks = functools.reduce(jnp.add, [blocks_ref[at] for at in range(16)])
    lane_place = lax.broadcasted_iota(jnp.int32, (8, 128), 1) >> 4

    def own_lanes(lanes):
        result = jnp.zeros((8, 128), f32)
        for q in range(8):
            rows = get(state, lanes, 8 * q, 8)
            rows = jnp.where(place >= 8, rows[:, 128:256], rows[:, 0:128])
            rows = pltpu.roll(rows, (16 * (q - place)) & 127, 1)
            result = jnp.where(lane_place == q, rows, result)
        return result

    start, mapped, residual = own_lanes(START), own_lanes(MAPPED), own_lanes(RESIDUAL)
    image = blocks[0:8] + damping * residual
    before, after = get(state, BEFORE, 0, 56), get(state, AFTER, 0, 64)
    norm_first = jnp.sum(before[48:56])
    product_first = jnp.max(get(state, SCALAR, 0, 8))
    alpha_first = norm_first / product_first
    norm_now = jnp.sum(after[48:56])
    crossed = jnp.sum(after[56:64])
    beta = norm_now / norm_first
    product = jnp.sum(blocks[8:16]) + damping * norm_now + beta * (2.0 * crossed + beta * product_first)
    alpha = norm_now / product
    from_start = alpha_first + alpha * beta
    solution = from_start * start + alpha * residual
    left = residual - alpha * (image + beta * mapped)
    both = split_rows(jnp.concatenate([solution, left], axis=0))
    held = lax.broadcasted_iota(jnp.int32, (128, 256), 0)
    wanted = lax.broadcasted_iota(jnp.int32, (128, 256), 1)
    same = (held & 15) == (wanted >> 4)
    halves = [
        join_rows(dot_nn(both, jnp.where(same & ((wanted & 15) == 2 * (held >> 4) + upper), 1.0, 0.0).astype(bf16)))
        for upper in range(2)
    ]
    for at, ref in enumerate((solution_ref, left_ref)):
        own_rows = halves[0][8 * at : 8 * at + 4] + halves[1][8 * at + 4 : 8 * at + 8]
        for c in range(4):
            ref[c] = own_rows[c : c + 1]
    rhs = get(state, FACTOR_B, 40, 40)
    target = [tile(rhs, j) - from_start * tile(before, j) - alpha * tile(after, j) for j in range(5)]
    solved = chol_solve(kept_factor(state), target)
    for j in range(5):
        for a in range(8):
            source_ref[j : j + 1, 128 * a : 128 * a + 128] = solved[j][a : a + 1]


VMEM = pl.BlockSpec(memory_space=pltpu.VMEM)
SMEM = pl.BlockSpec(memory_space=pltpu.SMEM)


def call(kernel, name, outs, *operands, scalars=0, aliases=None, work_ahead=0):
    specs = [SMEM] * scalars + [VMEM] * (len(operands) - scalars)
    shapes = [jax.ShapeDtypeStruct(shape, dtype) for shape, dtype in outs]
    return pl.pallas_call(
        kernel,
        out_shape=shapes,
        in_specs=specs,
        out_specs=[VMEM] * len(outs),
        input_output_aliases=aliases or {},
        compiler_params=pltpu.CompilerParams(vmem_limit_bytes=8 * 1024 * 1024),
        cost_estimate=pl.CostEstimate(flops=work_ahead, bytes_accessed=0, transcendentals=0) if work_ahead else None,
        name=name,
    )(*operands)


def ring_parts(value, axis):
    count = lax.axis_size(axis)
    return [value] + [
        lax.ppermute(value, axis, [(at, (at + step) % count) for at in range(count)]) for step in (1, 2, 3)
    ]


def crossing(value, step):
    chips = lax.axis_size("tm_0")
    pairs = [(2 * at + core, 2 * ((at + step) % chips) + 1 - core) for at in range(chips) for core in range(2)]
    return lax.ppermute(value, TM, pairs)


def to_twin(value):
    return lax.ppermute(value, "tm_1", [(0, 1), (1, 0)])


def tm_parts(value):
    value = value + to_twin(value)
    return ring_parts(value, "tm_0")


def sky_parts(knots):
    own, one, two, three = ring_parts(knots, "sky_1")
    return ring_parts((own + two) + (one + three), "sky_0")


KNOTS = ((80, 256), f32)
GHOSTS = ((48, 128), f32)


def shards(obs_source, obs_knot, obs_count, src_design, att_design, obs_phase, obs_value, src_prior):
    at = lax.axis_index(TM)
    first = (at == 0).astype(jnp.int32).reshape(1)
    last = (at == lax.axis_size(TM) - 1).astype(jnp.int32).reshape(1)
    tm = at.astype(jnp.int32).reshape(1)
    place = lax.axis_index(SKY).astype(jnp.int32).reshape(1)
    line = lambda value: value.reshape(1, OBS_DEV)
    (state,) = call(open_kernel, "open", [STATE], work_ahead=1 << 32)
    work, sums, state = call(
        source_kernel,
        "source_sums",
        [WORK, ((160, 128), f32), STATE],
        obs_count, first, line(obs_source), src_design, line(obs_value), src_prior, state,
        aliases={6: 2},
        scalars=2,
    )
    twin_sums = to_twin(sums)
    (work,) = call(
        knot_kernel,
        "knot_spread",
        [WORK],
        obs_count, last, line(obs_knot), att_design, line(obs_phase), work,
        scalars=2,
        aliases={5: 0},
    )
    earlier, later, twin = call(
        ghost_kernel,
        "ghosts",
        [GHOSTS] * 3,
        obs_count, tm, obs_knot.reshape(32, 128), line(obs_source), src_design, work,
        scalars=2,
    )
    sums = sums + twin_sums
    onward = jnp.concatenate([sums, later], axis=0)
    parts = (
        onward,
        crossing(onward, 1),
        lax.ppermute(sums, "tm_0", [(at, (at + 2) % 4) for at in range(4)]),
        crossing(jnp.concatenate([sums, earlier], axis=0), -1),
        to_twin(twin),
    )
    knots, work, state = call(
        first_kernel, "first", [KNOTS, WORK, STATE], tm, *parts, work, state, scalars=1, aliases={6: 1, 7: 2}
    )
    parts = sky_parts(knots)
    kept = dict(scalars=1, aliases={5: 1, 6: 2})
    sums, work, state = call(start_kernel, "start", [((64, 128), f32), WORK, STATE], tm, *parts, work, state, **kept)
    parts = tm_parts(sums)
    knots, work, state = call(back_kernel, "back", [KNOTS, WORK, STATE], tm, *parts, work, state, **kept)
    parts = sky_parts(knots)
    sums, work, state = call(next_kernel, "next", [((72, 128), f32), WORK, STATE], tm, *parts, work, state, **kept)
    parts = tm_parts(sums)
    blocks, work, state = call(
        back_to_owners_kernel, "back_to_owners", [((16, 16, 128), f32), WORK, STATE], tm, *parts, work, state, **kept
    )
    blocks = lax.all_to_all(blocks, SKY, 0, 0, tiled=True)
    return call(
        last_kernel,
        "last",
        [((4, 1, 256), f32), ((4, 1, 256), f32), ((5, 1024), f32)],
        place, blocks, state,
        scalars=1,
    )


def solution(mesh):
    torus = Mesh(mesh.devices.reshape(4, 4, 4, 2), SKY_TM)
    placed = (
        P(SKY_TM),
        P(SKY_TM),
        P(SKY_TM),
        P(None, SKY_TM),
        P(None, SKY_TM),
        P(SKY_TM),
        P(SKY_TM),
        P(None, SKY),
    )
    return jax.shard_map(
        shards,
        mesh=torus,
        in_specs=placed,
        out_specs=(P(None, TM, SKY), P(None, TM, SKY), P(None, SKY)),
        check_vma=False,
    )
```

```python
import functools

import jax
import jax.numpy as jnp
from jax import lax
from jax.experimental import pallas as pl
from jax.experimental.pallas import tpu as pltpu
from jax.sharding import Mesh
from jax.sharding import PartitionSpec as P

SKY = ("sky_0", "sky_1")
TM = ("tm_0", "tm_1")
SKY_TM = ("sky_0", "sky_1", "tm_0", "tm_1")

OBS_DEV = 4096
CHUNK = 4096
damping = 0.5
entry_pairs = [(row_at, col_at) for row_at in range(5) for col_at in range(row_at + 1)]


f32 = jnp.float32
bf16 = jnp.bfloat16


def split_rows(value):
    first = value.astype(bf16)
    rest = value - first.astype(f32)
    second = rest.astype(bf16)
    third = (rest - second.astype(f32)).astype(bf16)
    return jnp.concatenate([first, second, third], axis=0)


def join_rows(stacked):
    rows = stacked.shape[0] // 3
    return stacked[:rows] + (stacked[rows : 2 * rows] + stacked[2 * rows :])


def dot_nt(left, right):
    return lax.dot_general(left, right, (((1,), (1,)), ((), ())), preferred_element_type=f32)


def dot_nn(left, right):
    return lax.dot_general(left, right, (((1,), (0,)), ((), ())), preferred_element_type=f32)


def chunks():
    return [slice(start, start + CHUNK) for start in range(0, OBS_DEV, CHUNK)]


def four(refs):
    own, one, three, two = (ref[...] for ref in refs)
    return (own + two) + (one + three)


def lanes_from(start, rows):
    return lax.broadcasted_iota(jnp.int32, (rows, CHUNK), 1) + start


SOURCE_SPREAD = slice(0, 40)
KNOT_SPREAD = slice(40, 120)
IMAGE = slice(120, 121)
SOURCE_LANE = slice(121, 122)
KNOT_LANE = slice(122, 123)
START, MAPPED, RESIDUAL = (slice(at, at + 256) for at in (0, 256, 512))
FACTOR_A, FACTOR_B, BEFORE, AFTER, SCALAR = (slice(at, at + 128) for at in (768, 896, 1024, 1152, 1280))
WORK = ((128, OBS_DEV), f32)
STATE = ((80, 1408), f32)


def put(state, lanes, start, value):
    state[start : start + value.shape[0], lanes] = value


def get(state, lanes, start, rows):
    return state[start : start + rows, lanes]


GHOST_PLACES = ((SCALAR, 8), (SCALAR, 32), (SCALAR, 56), (BEFORE, 56))


def put_ghosts(state, ghosts):
    for at, (lanes, start) in enumerate(GHOST_PLACES):
        put(state, lanes, start, ghosts[:, 128 * at : 128 * at + 128])


def get_ghosts(state):
    return jnp.concatenate([get(state, lanes, start, 24) for lanes, start in GHOST_PLACES], axis=1)


def row_numbers(rows, lanes=CHUNK):
    return lax.broadcasted_iota(jnp.int32, (rows, lanes), 0).astype(f32).astype(bf16)


def hot_rows(numbers, lane_row):
    wanted = jnp.broadcast_to(lane_row, numbers.shape).astype(bf16)
    return jnp.where(numbers == wanted, jnp.ones_like(numbers), jnp.zeros_like(numbers))


def open_kernel(state):
    state[0:8, 0:128] = jnp.zeros((8, 128), f32)


def source_kernel(count_ref, first_ref, source_ref, g_ref, y_ref, prior_ref, _state, work, sums_ref, state):
    numbers = row_numbers(128)
    total = jnp.zeros((480, 128), f32)
    for at in chunks():
        live = lanes_from(at.start, 1) < count_ref[0]
        source = source_ref[:, at]
        lane = (source & 127).astype(f32)
        work[SOURCE_LANE, at] = lane
        mark = jnp.where(live, source >> 7, -1)
        chosen = jnp.where(lax.broadcasted_iota(jnp.int32, (8, CHUNK), 0) == mark, 1.0, 0.0)
        g = [g_ref[j : j + 1, at] for j in range(5)]
        y = y_ref[:, at]
        work[IMAGE, at] = y
        spread = [chosen * g[j] for j in range(5)]
        for j in range(5):
            work[8 * j : 8 * j + 8, at] = spread[j]
        rows = [spread[r] * g[c] for r, c in entry_pairs] + [spread[j] * y for j in range(5)]
        total = total + dot_nt(split_rows(jnp.concatenate(rows, axis=0)), hot_rows(numbers, lane))
    sums_ref[...] = join_rows(total)
    once = jnp.where(first_ref[0] == 1, 1.0, 0.0)
    for at, (row_at, col_at) in enumerate(entry_pairs):
        if row_at == col_at:
            prior = jnp.concatenate([prior_ref[row_at : row_at + 1, 128 * a : 128 * a + 128] for a in range(8)], axis=0)
            sums_ref[8 * at : 8 * at + 8] += prior * once


def knot_kernel(count_ref, last_ref, knot_ref, h_ref, phase_ref, _work, work):
    upper = lax.broadcasted_iota(jnp.int32, (8, CHUNK), 0) >> 2
    for at in chunks():
        live = lanes_from(at.start, 1) < count_ref[0]
        knot = knot_ref[:, at]
        high = knot >> 4
        work[KNOT_LANE, at] = high.astype(f32)
        h = jnp.where(live, h_ref[:, at], 0.0)
        h = jnp.concatenate([h, h], axis=0)
        phase = phase_ref[:, at]
        squared = phase * phase
        cubed = squared * phase
        rest = 1.0 - phase
        taps = (
            rest * rest * rest / 6.0,
            (3.0 * cubed - 6.0 * squared + 4.0) / 6.0,
            (-3.0 * cubed + 3.0 * squared + 3.0 * phase + 1.0) / 6.0,
            cubed / 6.0,
        )
        taps = [jnp.broadcast_to(tap, (8, CHUNK)) for tap in taps]
        ahead = upper - (knot & 15)
        kept = jnp.where((high == 255) & (last_ref[0] == 1), 0.0, 1.0)
        for q in range(10):
            gap = ahead + 2 * q
            weight = jnp.where(gap == 0, taps[0], 0.0)
            for m in range(1, 4):
                weight = jnp.where(gap == m, taps[m], weight)
            if q >= 8:
                weight = weight * kept
            row = KNOT_SPREAD.start + 8 * q
            work[row : row + 8, at] = weight * h


def ghost_kernel(count_ref, tm_ref, flat_ref, source_ref, g_ref, work, earlier_ref, later_ref, twin_ref):
    knot = flat_ref[...]
    order = lax.broadcasted_iota(jnp.int32, (32, 128), 0) * 128 + lax.broadcasted_iota(jnp.int32, (32, 128), 1)
    live = order < count_ref[0]
    across = jnp.where(
        lax.broadcasted_iota(jnp.int32, (128, 128), 0) < lax.broadcasted_iota(jnp.int32, (128, 128), 1), 1.0, 0.0
    ).astype(bf16)
    down = jnp.where(
        lax.broadcasted_iota(jnp.int32, (32, 32), 0) > lax.broadcasted_iota(jnp.int32, (32, 32), 1), 1.0, 0.0
    ).astype(bf16)
    numbers = row_numbers(256, 128)
    at_low = live & (knot < 3) & (tm_ref[0] > 0)
    for chosen, spread_at, ref in ((live & (knot >= 4093), 104, later_ref), (at_low, 40, earlier_ref)):
        mark = jnp.where(chosen, 1.0, 0.0).astype(bf16)
        rank = dot_nn(mark, across) + jnp.sum(dot_nn(down, mark), axis=1, keepdims=True)
        rank = jnp.where(chosen, rank, -1.0)
        total = jnp.zeros((72, 256), f32)
        for at in chunks():
            first = at.start // 128
            slots = jnp.concatenate([hot_rows(numbers, rank[row : row + 1]) for row in range(first, first + CHUNK // 128)], axis=1)
            data = jnp.concatenate(
                [work[spread_at : spread_at + 16, at], g_ref[:, at], source_ref[:, at].astype(f32), work[IMAGE, at], jnp.zeros((1, CHUNK), f32)],
                axis=0,
            )
            total = total + dot_nt(split_rows(data), slots)
        total = join_rows(total)
        ref[0:24] = total[:, 0:128]
        ref[24:48] = total[:, 128:256]
    twin_ref[...] = jnp.where((tm_ref[0] & 1) == 1, earlier_ref[...], later_ref[...])


def ghost_sums(solved, ghosts, values):
    source = ghosts[21:22].astype(jnp.int32)
    picked = join_rows(dot_nn(solved, hot_rows(row_numbers(128, 512), (source & 127).astype(f32))))
    fitted = functools.reduce(jnp.add, [tile(picked, j) * ghosts[16 + j : 17 + j] for j in range(5)])
    fitted = jnp.where(lax.broadcasted_iota(jnp.int32, (8, 512), 0) == (source >> 7), fitted, 0.0)
    weighted = ghosts[0:16] * (values - jnp.sum(fitted, axis=0, keepdims=True))
    return jnp.sum(weighted[:, 0:256], axis=1, keepdims=True), jnp.sum(weighted[:, 256:512], axis=1, keepdims=True)


def end_tile(at_tm, high, low):
    lane = lax.broadcasted_iota(jnp.int32, (8, 128), 1)
    result = jnp.zeros((8, 128), f32)
    for place, part in enumerate((high[0:8], high[8:16], low[0:8], low[8:16])):
        result = jnp.where(lane == at_tm + 16 * place, part, result)
    return result


def end_parts(at_tm, ends):
    lane = lax.broadcasted_iota(jnp.int32, (8, 128), 1)
    pick = lambda at: jnp.sum(jnp.where(lane == at, ends, 0.0), axis=1, keepdims=True)
    earlier = jnp.concatenate([pick(at_tm - 1), pick(at_tm + 15)], axis=0)
    later = jnp.concatenate([pick(at_tm + 33), pick(at_tm + 49)], axis=0)
    return earlier, later


def tile(value, at):
    return value[8 * at : 8 * at + 8]


def factor_of(value):
    return {pair: tile(value, at) for at, pair in enumerate(entry_pairs)}


def factorize(normal):
    factor = {}
    for row_at in range(5):
        for col_at in range(row_at + 1):
            running = normal[row_at, col_at]
            for inner_at in range(col_at):
                running = running - factor[row_at, inner_at] * factor[col_at, inner_at]
            if row_at == col_at:
                factor[row_at, row_at] = 1.0 / jnp.sqrt(running)
            else:
                factor[row_at, col_at] = running * factor[col_at, col_at]
    return factor


def chol_solve(factor, target):
    forward = []
    for row_at in range(5):
        running = target[row_at]
        for inner_at in range(row_at):
            running = running - factor[row_at, inner_at] * forward[inner_at]
        forward.append(running * factor[row_at, row_at])
    result = [None] * 5
    for row_at in reversed(range(5)):
        running = forward[row_at]
        for inner_at in range(row_at + 1, 5):
            running = running - factor[inner_at, row_at] * result[inner_at]
        result[row_at] = running * factor[row_at, row_at]
    return result


def eliminate_and_spread(solved, work):
    source_numbers, knot_numbers = row_numbers(128), row_numbers(256)
    total = jnp.zeros((240, 256), f32)
    for at in chunks():
        picked = join_rows(dot_nn(solved, hot_rows(source_numbers, work[SOURCE_LANE, at])))
        fitted = jnp.sum(picked * work[SOURCE_SPREAD, at], axis=0, keepdims=True)
        cleaned = work[IMAGE, at] - fitted
        total = total + dot_nt(split_rows(work[KNOT_SPREAD, at] * cleaned), hot_rows(knot_numbers, work[KNOT_LANE, at]))
    return join_rows(total)


def with_ends(total, earlier, later, energy):
    lane = lax.broadcasted_iota(jnp.int32, (16, 256), 1)
    within = lax.broadcasted_iota(jnp.int32, (16, 256), 0) < 12
    beyond = jnp.where(within, total[64:80], 0.0)
    low = total[0:16] + jnp.where(lane == 0, jnp.where(within, earlier, 0.0), pltpu.roll(beyond, 1, 1))
    after_end = beyond[:, 255:256] + jnp.where(lax.broadcasted_iota(jnp.int32, (16, 1), 0) < 12, later, 0.0)
    lane = lax.broadcasted_iota(jnp.int32, (8, 128), 1)
    beside = jnp.where(lane == 0, after_end[0:8], jnp.where(lane == 1, after_end[8:16], 0.0))
    return jnp.concatenate([low, total[16:64], jnp.concatenate([energy, beside], axis=1)], axis=0)


def first_kernel(tm_ref, own, one, three, two, twin, _work, _state, knots_ref, work, state):
    sums = (own[0:160] + two[...]) + (one[0:160] + three[0:160])
    odd = (tm_ref[0] & 1) == 1
    earlier = jnp.where(odd, twin[...], one[160:208])
    later = jnp.where(odd, three[160:208], twin[...])
    factor = factorize(factor_of(sums))
    stacked = jnp.concatenate([factor[pair] for pair in entry_pairs], axis=0)
    put(state, FACTOR_A, 0, stacked[0:80])
    put(state, FACTOR_B, 0, stacked[80:120])
    put(state, FACTOR_B, 40, sums[120:160])
    ghosts = jnp.concatenate([earlier[0:24], earlier[24:48], later[0:24], later[24:48]], axis=1)
    put_ghosts(state, ghosts)
    solved = split_rows(jnp.concatenate(chol_solve(factor, [tile(sums, 15 + j) for j in range(5)]), axis=0))
    earlier, later = ghost_sums(solved, ghosts, ghosts[22:23])
    knots_ref[...] = with_ends(eliminate_and_spread(solved, work), earlier, later, jnp.zeros((8, 128), f32))


def kept_factor(state):
    return factor_of(jnp.concatenate([get(state, FACTOR_A, 0, 80), get(state, FACTOR_B, 0, 40)], axis=0))


def back(lanes, at_tm, parts, work, state):
    sums = four(parts)
    put(state, lanes, 0, sums[:-8])
    target = [tile(sums, j) for j in range(5)]
    solved = chol_solve(kept_factor(state), target)
    energy = jnp.where(lax.broadcasted_iota(jnp.int32, (8, 128), 0) == 0, tile(sums, 5), 0.0)
    for j in range(5):
        energy = energy - target[j] * solved[j]
    solved = split_rows(jnp.concatenate(solved, axis=0))
    ends = zip(ghost_sums(solved, get_ghosts(state), 0.0), end_parts(at_tm, sums[-8:]))
    earlier, later = (ghost + image for ghost, image in ends)
    return with_ends(eliminate_and_spread(solved, work), earlier, later, energy), energy


def back_kernel(tm_ref, own, one, three, two, _work, _state, knots_ref, work, state):
    knots_ref[...], _ = back(BEFORE, tm_ref[0], (own, one, three, two), work, state)


def back_to_owners_kernel(tm_ref, own, one, three, two, _work, _state, blocks_ref, work, state):
    knots, energy = back(AFTER, tm_ref[0], (own, one, three, two), work, state)
    group = lax.broadcasted_iota(jnp.int32, (8, 128), 1) >> 4
    for half in range(2):
        tiles = [knots[8 * q : 8 * q + 8, 128 * half : 128 * half + 128] for q in range(8)]
        for stage in (1, 2, 4):
            at_first = (group & stage) == 0
            for q in range(8):
                if q & stage == 0:
                    here, there = tiles[q], tiles[q + stage]
                    tiles[q] = jnp.where(at_first, here, pltpu.roll(there, 16 * stage, 1))
                    tiles[q + stage] = jnp.where(at_first, pltpu.roll(here, 128 - 16 * stage, 1), there)
        for at in range(8):
            blocks_ref[8 * half + at, 0:8] = tiles[at]
            blocks_ref[8 * half + at, 8:16] = energy


def assembled(knots):
    lane = lax.broadcasted_iota(jnp.int32, (16, 256), 1)
    row = lax.broadcasted_iota(jnp.int32, (16, 256), 0)
    after_end = jnp.concatenate([knots[64:72, 128:129], knots[64:72, 129:130]], axis=0)
    following = jnp.where(lane == 255, after_end, pltpu.roll(knots[0:16], 255, 1))
    return jnp.concatenate([knots[0:64], jnp.where(row < 12, following, 0.0)], axis=0)


def energy_of(knots):
    return jnp.sum(knots[64:72, 0:128])


def folded(left, right):
    product = left[0:64] * right[0:64]
    return jnp.sum(product[:, 0:128] + product[:, 128:256], axis=0, keepdims=True)


def lane_blocks(value):
    return functools.reduce(jnp.add, [value[:, start : start + 128] for start in range(0, CHUNK, 128)])


def gather_and_sum(at_tm, field, work):
    source_numbers, knot_numbers = row_numbers(128), row_numbers(256)
    parts = split_rows(field)
    total = jnp.zeros((120, 128), f32)
    square = jnp.zeros((1, 128), f32)
    high = jnp.zeros((16, 128), f32)
    low = jnp.zeros((16, 128), f32)
    for at in chunks():
        knot_lane = work[KNOT_LANE, at]
        picked = join_rows(dot_nn(parts, hot_rows(knot_numbers, knot_lane)))
        image = jnp.sum(picked * work[KNOT_SPREAD, at], axis=0, keepdims=True)
        work[IMAGE, at] = image
        square = square + lane_blocks(image * image)
        high = high + lane_blocks(work[104:120, at] * jnp.where(knot_lane == 255.0, image, 0.0))
        low = low + lane_blocks(work[40:56, at] * jnp.where(knot_lane == 0.0, image, 0.0))
        total = total + dot_nt(split_rows(work[SOURCE_SPREAD, at] * image), hot_rows(source_numbers, work[SOURCE_LANE, at]))
    ends = end_tile(at_tm, jnp.sum(high, axis=1, keepdims=True), jnp.sum(low, axis=1, keepdims=True))
    return join_rows(total), square, ends


def start_kernel(tm_ref, own, one, three, two, _work, _state, sums_ref, work, state):
    residual = assembled(four((own, one, three, two)))
    put(state, START, 0, residual)
    sums, square, ends = gather_and_sum(tm_ref[0], residual, work)
    norm = folded(residual, residual)
    sums_ref[...] = jnp.concatenate([sums, square, norm, jnp.zeros((6, 128), f32), ends], axis=0)


def next_kernel(tm_ref, own, one, three, two, _work, _state, sums_ref, work, state):
    knots = four((own, one, three, two))
    direction = get(state, START, 0, 80)
    mapped = assembled(knots) + damping * direction
    norm_now = jnp.sum(get(state, BEFORE, 41, 1))
    product = energy_of(knots) + damping * norm_now
    residual = direction - (norm_now / product) * mapped
    put(state, MAPPED, 0, mapped)
    put(state, RESIDUAL, 0, residual)
    put(state, SCALAR, 0, jnp.zeros((8, 128), f32) + product)
    sums, square, ends = gather_and_sum(tm_ref[0], residual, work)
    norm, crossed = folded(residual, residual), folded(residual, mapped)
    sums_ref[...] = jnp.concatenate([sums, square, norm, crossed, jnp.zeros((5, 128), f32), ends], axis=0)


OWN = ((152, 128), f32)


def own_kernel(place_ref, state, own_ref):
    place = place_ref[0]
    lane_place = lax.broadcasted_iota(jnp.int32, (8, 128), 1) >> 4
    for at, lanes in enumerate((START, MAPPED, RESIDUAL)):
        result = jnp.zeros((8, 128), f32)
        for q in range(8):
            rows = get(state, lanes, 8 * q, 8)
            rows = jnp.where(place >= 8, rows[:, 128:256], rows[:, 0:128])
            rows = pltpu.roll(rows, (16 * (q - place)) & 127, 1)
            result = jnp.where(lane_place == q, rows, result)
        own_ref[8 * at : 8 * at + 8] = result
    factor = kept_factor(state)
    for at, value in enumerate((get(state, FACTOR_B, 40, 40), get(state, BEFORE, 0, 40), get(state, AFTER, 0, 40))):
        start = 24 + 40 * at
        own_ref[start : start + 40] = jnp.concatenate(chol_solve(factor, [tile(value, j) for j in range(5)]), axis=0)
    norm_first = jnp.sum(get(state, BEFORE, 41, 1))
    norm_now = jnp.sum(get(state, AFTER, 41, 1))
    crossed = jnp.sum(get(state, AFTER, 42, 1))
    product_first = jnp.max(get(state, SCALAR, 0, 8))
    alpha_first = norm_first / product_first
    beta = norm_now / norm_first
    product = damping * norm_now + beta * (2.0 * crossed + beta * product_first)
    row = lax.broadcasted_iota(jnp.int32, (8, 128), 0)
    scalars = jnp.zeros((8, 128), f32)
    for at, value in enumerate((alpha_first, beta, norm_now, product)):
        scalars = jnp.where(row == at, value, scalars)
    own_ref[144:152] = scalars


def last_kernel(blocks_ref, own_ref, solution_ref, left_ref, source_ref):
    blocks = functools.reduce(jnp.add, [blocks_ref[at] for at in range(16)])
    start, mapped, residual = own_ref[0:8], own_ref[8:16], own_ref[16:24]
    alpha_first, beta, norm_now, product = (own_ref[144 + at : 145 + at] for at in range(4))
    alpha = norm_now / (jnp.sum(blocks[8:16]) + product)
    from_start = alpha_first + alpha * beta
    image = blocks[0:8] + damping * residual
    solution = from_start * start + alpha * residual
    left = residual - alpha * (image + beta * mapped)
    both = split_rows(jnp.concatenate([solution, left], axis=0))
    held = lax.broadcasted_iota(jnp.int32, (128, 256), 0)
    wanted = lax.broadcasted_iota(jnp.int32, (128, 256), 1)
    same = (held & 15) == (wanted >> 4)
    halves = [
        join_rows(dot_nn(both, jnp.where(same & ((wanted & 15) == 2 * (held >> 4) + upper), 1.0, 0.0).astype(bf16)))
        for upper in range(2)
    ]
    for at, ref in enumerate((solution_ref, left_ref)):
        own_rows = halves[0][8 * at : 8 * at + 4] + halves[1][8 * at + 4 : 8 * at + 8]
        for c in range(4):
            ref[c] = own_rows[c : c + 1]
    for j in range(5):
        plain, before, after = (own_ref[start + 8 * j : start + 8 * j + 8] for start in (24, 64, 104))
        solved = plain - from_start * before - alpha * after
        for a in range(8):
            source_ref[j : j + 1, 128 * a : 128 * a + 128] = solved[a : a + 1]


VMEM = pl.BlockSpec(memory_space=pltpu.VMEM)
SMEM = pl.BlockSpec(memory_space=pltpu.SMEM)


def call(kernel, name, outs, *operands, scalars=0, aliases=None, work_ahead=0):
    specs = [SMEM] * scalars + [VMEM] * (len(operands) - scalars)
    shapes = [jax.ShapeDtypeStruct(shape, dtype) for shape, dtype in outs]
    return pl.pallas_call(
        kernel,
        out_shape=shapes,
        in_specs=specs,
        out_specs=[VMEM] * len(outs),
        input_output_aliases=aliases or {},
        compiler_params=pltpu.CompilerParams(vmem_limit_bytes=8 * 1024 * 1024),
        cost_estimate=pl.CostEstimate(flops=work_ahead, bytes_accessed=0, transcendentals=0) if work_ahead else None,
        name=name,
    )(*operands)


def ring_parts(value, axis):
    count = lax.axis_size(axis)
    return [value] + [
        lax.ppermute(value, axis, [(at, (at + step) % count) for at in range(count)]) for step in (1, 3, 2)
    ]


def crossing(value, step):
    chips = lax.axis_size("tm_0")
    pairs = [(2 * at + core, 2 * ((at + step) % chips) + 1 - core) for at in range(chips) for core in range(2)]
    return lax.ppermute(value, TM, pairs)


def to_twin(value):
    return lax.ppermute(value, "tm_1", [(0, 1), (1, 0)])


def tm_parts(value):
    value = value + to_twin(value)
    return ring_parts(value, "tm_0")


def sky_parts(knots):
    own, one, three, two = ring_parts(knots, "sky_1")
    return ring_parts((one + three) + (two + own), "sky_0")


KNOTS = ((72, 256), f32)
GHOSTS = ((48, 128), f32)
SUMS = ((56, 128), f32)


def shards(obs_source, obs_knot, obs_count, src_design, att_design, obs_phase, obs_value, src_prior):
    at = lax.axis_index(TM)
    first = (at == 0).astype(jnp.int32).reshape(1)
    last = (at == lax.axis_size(TM) - 1).astype(jnp.int32).reshape(1)
    tm = at.astype(jnp.int32).reshape(1)
    place = lax.axis_index(SKY).astype(jnp.int32).reshape(1)
    line = lambda value: value.reshape(1, OBS_DEV)
    (state,) = call(open_kernel, "open", [STATE], work_ahead=1 << 32)
    work, sums, state = call(
        source_kernel,
        "source_sums",
        [WORK, ((160, 128), f32), STATE],
        obs_count, first, line(obs_source), src_design, line(obs_value), src_prior, state,
        aliases={6: 2},
        scalars=2,
    )
    twin_sums = to_twin(sums)
    (work,) = call(
        knot_kernel,
        "knot_spread",
        [WORK],
        obs_count, last, line(obs_knot), att_design, line(obs_phase), work,
        scalars=2,
        aliases={5: 0},
    )
    earlier, later, twin = call(
        ghost_kernel,
        "ghosts",
        [GHOSTS] * 3,
        obs_count, tm, obs_knot.reshape(32, 128), line(obs_source), src_design, work,
        scalars=2,
    )
    sums = sums + twin_sums
    onward = jnp.concatenate([sums, later], axis=0)
    parts = (
        onward,
        crossing(onward, 1),
        crossing(jnp.concatenate([sums, earlier], axis=0), -1),
        lax.ppermute(sums, "tm_0", [(at, (at + 2) % 4) for at in range(4)]),
        to_twin(twin),
    )
    knots, work, state = call(
        first_kernel, "first", [KNOTS, WORK, STATE], tm, *parts, work, state, scalars=1, aliases={6: 1, 7: 2}
    )
    parts = sky_parts(knots)
    kept = dict(scalars=1, aliases={5: 1, 6: 2})
    sums, work, state = call(start_kernel, "start", [SUMS, WORK, STATE], tm, *parts, work, state, **kept)
    parts = tm_parts(sums)
    knots, work, state = call(back_kernel, "back", [KNOTS, WORK, STATE], tm, *parts, work, state, **kept)
    parts = sky_parts(knots)
    sums, work, state = call(next_kernel, "next", [SUMS, WORK, STATE], tm, *parts, work, state, **kept)
    parts = tm_parts(sums)
    blocks, work, state = call(
        back_to_owners_kernel, "back_to_owners", [((16, 16, 128), f32), WORK, STATE], tm, *parts, work, state, **kept
    )
    (own,) = call(own_kernel, "own", [OWN], place, state, scalars=1)
    blocks = lax.all_to_all(blocks, SKY, 0, 0, tiled=True)
    return call(
        last_kernel,
        "last",
        [((4, 1, 256), f32), ((4, 1, 256), f32), ((5, 1024), f32)],
        blocks, own,
    )


def solution(mesh):
    torus = Mesh(mesh.devices.reshape(4, 4, 4, 2), SKY_TM)
    placed = (
        P(SKY_TM),
        P(SKY_TM),
        P(SKY_TM),
        P(None, SKY_TM),
        P(None, SKY_TM),
        P(SKY_TM),
        P(SKY_TM),
        P(None, SKY),
    )
    return jax.shard_map(
        shards,
        mesh=torus,
        in_specs=placed,
        out_specs=(P(None, TM, SKY), P(None, TM, SKY), P(None, SKY)),
        check_vma=False,
    )
```

```python
import functools

import jax
import jax.numpy as jnp
from jax import lax
from jax.experimental import pallas as pl
from jax.experimental.pallas import tpu as pltpu
from jax.sharding import Mesh
from jax.sharding import PartitionSpec as P

SKY = ("sky_0", "sky_1")
TM = ("tm_0", "tm_1")
SKY_TM = ("sky_0", "sky_1", "tm_0", "tm_1")

OBS_DEV = 4096
SEGMENTS = 8
CHUNK = 4096
damping = 0.5
entry_pairs = [(row_at, col_at) for row_at in range(5) for col_at in range(row_at + 1)]


f32 = jnp.float32
bf16 = jnp.bfloat16


def split_rows(value):
    first = value.astype(bf16)
    rest = value - first.astype(f32)
    second = rest.astype(bf16)
    third = (rest - second.astype(f32)).astype(bf16)
    return jnp.concatenate([first, second, third], axis=0)


def join_rows(stacked):
    rows = stacked.shape[0] // 3
    return stacked[:rows] + (stacked[rows : 2 * rows] + stacked[2 * rows :])


def dot_nt(left, right):
    return lax.dot_general(left, right, (((1,), (1,)), ((), ())), preferred_element_type=f32)


def dot_nn(left, right):
    return lax.dot_general(left, right, (((1,), (0,)), ((), ())), preferred_element_type=f32)


def chunks():
    return [slice(start, start + CHUNK) for start in range(0, OBS_DEV, CHUNK)]


def four(refs):
    own, one, three, two = (ref[...] for ref in refs)
    return (own + two) + (one + three)


def lanes_from(start, rows):
    return lax.broadcasted_iota(jnp.int32, (rows, CHUNK), 1) + start


SOURCE_SPREAD = slice(0, 40)
KNOT_SPREAD = slice(40, 120)
IMAGE = slice(120, 121)
SOURCE_LANE = slice(121, 122)
KNOT_LANE = slice(122, 123)
START, MAPPED, RESIDUAL = (slice(at, at + 256) for at in (0, 256, 512))
FACTOR_A, FACTOR_B, BEFORE, AFTER, SCALAR = (slice(at, at + 128) for at in (768, 896, 1024, 1152, 1280))
WORK = ((128, OBS_DEV), f32)
STATE = ((80, 1408), f32)


def put(state, lanes, start, value):
    state[start : start + value.shape[0], lanes] = value


def get(state, lanes, start, rows):
    return state[start : start + rows, lanes]


GHOST_PLACES = ((SCALAR, 8), (SCALAR, 32), (SCALAR, 56), (BEFORE, 56))


def put_ghosts(state, ghosts):
    for at, (lanes, start) in enumerate(GHOST_PLACES):
        put(state, lanes, start, ghosts[:, 128 * at : 128 * at + 128])


def get_ghosts(state):
    return jnp.concatenate([get(state, lanes, start, 24) for lanes, start in GHOST_PLACES], axis=1)


def row_numbers(rows, lanes=CHUNK):
    return lax.broadcasted_iota(jnp.int32, (rows, lanes), 0).astype(f32).astype(bf16)


def hot_rows(numbers, lane_row):
    wanted = jnp.broadcast_to(lane_row, numbers.shape).astype(bf16)
    return jnp.where(numbers == wanted, jnp.ones_like(numbers), jnp.zeros_like(numbers))


def open_kernel(state):
    state[0:8, 0:128] = jnp.zeros((8, 128), f32)


def source_kernel(count_ref, first_ref, source_ref, g_ref, y_ref, prior_ref, _state, work, sums_ref, state):
    numbers = row_numbers(128)
    total = jnp.zeros((480, 128), f32)
    for at in chunks():
        live = lanes_from(at.start, 1) < count_ref[0]
        source = source_ref[:, at]
        lane = (source & 127).astype(f32)
        work[SOURCE_LANE, at] = lane
        mark = jnp.where(live, source >> 7, -1)
        chosen = jnp.where(lax.broadcasted_iota(jnp.int32, (8, CHUNK), 0) == mark, 1.0, 0.0)
        g = [g_ref[j : j + 1, at] for j in range(5)]
        y = y_ref[:, at]
        work[IMAGE, at] = y
        spread = [chosen * g[j] for j in range(5)]
        for j in range(5):
            work[8 * j : 8 * j + 8, at] = spread[j]
        rows = [spread[r] * g[c] for r, c in entry_pairs] + [spread[j] * y for j in range(5)]
        total = total + dot_nt(split_rows(jnp.concatenate(rows, axis=0)), hot_rows(numbers, lane))
    sums_ref[...] = join_rows(total)
    once = jnp.where(first_ref[0] == 1, 1.0, 0.0)
    for at, (row_at, col_at) in enumerate(entry_pairs):
        if row_at == col_at:
            prior = jnp.concatenate([prior_ref[row_at : row_at + 1, 128 * a : 128 * a + 128] for a in range(8)], axis=0)
            sums_ref[8 * at : 8 * at + 8] += prior * once


def spline_taps(phase):
    squared = phase * phase
    cubed = squared * phase
    rest = 1.0 - phase
    return (
        rest * rest * rest / 6.0,
        (3.0 * cubed - 6.0 * squared + 4.0) / 6.0,
        (-3.0 * cubed + 3.0 * squared + 3.0 * phase + 1.0) / 6.0,
        cubed / 6.0,
    )


def tap_at(taps, gap):
    weight = jnp.where(gap == 0, taps[0], 0.0)
    for m in range(1, 4):
        weight = jnp.where(gap == m, taps[m], weight)
    return weight


def knot_kernel(count_ref, last_ref, knot_ref, h_ref, phase_ref, _work, work):
    upper = lax.broadcasted_iota(jnp.int32, (8, CHUNK), 0) >> 2
    for at in chunks():
        live = lanes_from(at.start, 1) < count_ref[0]
        knot = knot_ref[:, at]
        high = knot >> 4
        work[KNOT_LANE, at] = high.astype(f32)
        h = jnp.where(live, h_ref[:, at], 0.0)
        h = jnp.concatenate([h, h], axis=0)
        taps = [jnp.broadcast_to(tap, (8, CHUNK)) for tap in spline_taps(phase_ref[:, at])]
        ahead = upper - (knot & 15)
        kept = jnp.where((high == 255) & (last_ref[0] == 1), 0.0, 1.0)
        for q in range(10):
            weight = tap_at(taps, ahead + 2 * q)
            if q >= 8:
                weight = weight * kept
            row = KNOT_SPREAD.start + 8 * q
            work[row : row + 8, at] = weight * h


def ghost_kernel(count_ref, tm_ref, flat_ref, knot_ref, source_ref, g_ref, h_ref, phase_ref, work, earlier_ref, later_ref, twin_ref):
    knot = flat_ref[...]
    order = lax.broadcasted_iota(jnp.int32, (32, 128), 0) * 128 + lax.broadcasted_iota(jnp.int32, (32, 128), 1)
    live = order < count_ref[0]
    across = jnp.where(
        lax.broadcasted_iota(jnp.int32, (128, 128), 0) < lax.broadcasted_iota(jnp.int32, (128, 128), 1), 1.0, 0.0
    ).astype(bf16)
    down = jnp.where(
        lax.broadcasted_iota(jnp.int32, (32, 32), 0) > lax.broadcasted_iota(jnp.int32, (32, 32), 1), 1.0, 0.0
    ).astype(bf16)
    numbers = row_numbers(256, 128)
    at_low = live & (knot < 3) & (tm_ref[0] > 0)
    at_high = live & (knot >= 4093) & (tm_ref[0] < SEGMENTS - 1)
    totals = []
    for chosen, origin in ((at_high, 4096), (at_low, 0)):
        mark = jnp.where(chosen, 1.0, 0.0).astype(bf16)
        rank = dot_nn(mark, across) + jnp.sum(dot_nn(down, mark), axis=1, keepdims=True)
        rank = jnp.where(chosen, rank, -1.0)
        total = jnp.zeros((48, 256), f32)
        for at in chunks():
            first = at.start // 128
            slots = jnp.concatenate([hot_rows(numbers, rank[row : row + 1]) for row in range(first, first + CHUNK // 128)], axis=1)
            place = (knot_ref[:, at] - origin).astype(f32)
            data = jnp.concatenate(
                [g_ref[:, at], source_ref[:, at].astype(f32), work[IMAGE, at], phase_ref[:, at], place, h_ref[:, at], jnp.zeros((3, CHUNK), f32)],
                axis=0,
            )
            total = total + dot_nt(split_rows(data), slots)
        totals.append(join_rows(total))
    for total, ref in zip(totals, (later_ref, earlier_ref)):
        ref[0:16] = total[:, 0:128]
        ref[16:32] = total[:, 128:256]
    twin_ref[...] = jnp.where((tm_ref[0] & 1) == 1, earlier_ref[...], later_ref[...])


def unpacked(packed):
    taps = [jnp.broadcast_to(tap, (16, 512)) for tap in spline_taps(packed[7:8])]
    row = lax.broadcasted_iota(jnp.int32, (16, 512), 0)
    weight = tap_at(taps, (row >> 2) - packed[8:9].astype(jnp.int32))
    h = jnp.concatenate([packed[9:13]] * 4, axis=0)
    return jnp.concatenate([weight * h, packed[0:7], jnp.zeros((1, 512), f32)], axis=0)


def ghost_sums(solved, ghosts, values):
    source = ghosts[21:22].astype(jnp.int32)
    picked = join_rows(dot_nn(solved, hot_rows(row_numbers(128, 512), (source & 127).astype(f32))))
    fitted = functools.reduce(jnp.add, [tile(picked, j) * ghosts[16 + j : 17 + j] for j in range(5)])
    fitted = jnp.where(lax.broadcasted_iota(jnp.int32, (8, 512), 0) == (source >> 7), fitted, 0.0)
    weighted = ghosts[0:16] * (values - jnp.sum(fitted, axis=0, keepdims=True))
    return jnp.sum(weighted[:, 0:256], axis=1, keepdims=True), jnp.sum(weighted[:, 256:512], axis=1, keepdims=True)


def end_tile(at_tm, high, low):
    lane = lax.broadcasted_iota(jnp.int32, (8, 128), 1)
    result = jnp.zeros((8, 128), f32)
    for place, part in enumerate((high[0:8], high[8:16], low[0:8], low[8:16])):
        result = jnp.where(lane == at_tm + 16 * place, part, result)
    return result


def end_parts(at_tm, ends):
    lane = lax.broadcasted_iota(jnp.int32, (8, 128), 1)
    pick = lambda at: jnp.sum(jnp.where(lane == at, ends, 0.0), axis=1, keepdims=True)
    earlier = jnp.concatenate([pick(at_tm - 1), pick(at_tm + 15)], axis=0)
    later = jnp.concatenate([pick(at_tm + 33), pick(at_tm + 49)], axis=0)
    return earlier, later


def tile(value, at):
    return value[8 * at : 8 * at + 8]


def factor_of(value):
    return {pair: tile(value, at) for at, pair in enumerate(entry_pairs)}


def factorize(normal):
    factor = {}
    for row_at in range(5):
        for col_at in range(row_at + 1):
            running = normal[row_at, col_at]
            for inner_at in range(col_at):
                running = running - factor[row_at, inner_at] * factor[col_at, inner_at]
            if row_at == col_at:
                factor[row_at, row_at] = 1.0 / jnp.sqrt(running)
            else:
                factor[row_at, col_at] = running * factor[col_at, col_at]
    return factor


def chol_solve(factor, target):
    forward = []
    for row_at in range(5):
        running = target[row_at]
        for inner_at in range(row_at):
            running = running - factor[row_at, inner_at] * forward[inner_at]
        forward.append(running * factor[row_at, row_at])
    result = [None] * 5
    for row_at in reversed(range(5)):
        running = forward[row_at]
        for inner_at in range(row_at + 1, 5):
            running = running - factor[inner_at, row_at] * result[inner_at]
        result[row_at] = running * factor[row_at, row_at]
    return result


def eliminate_and_spread(solved, work):
    source_numbers, knot_numbers = row_numbers(128), row_numbers(256)
    total = jnp.zeros((240, 256), f32)
    for at in chunks():
        picked = join_rows(dot_nn(solved, hot_rows(source_numbers, work[SOURCE_LANE, at])))
        fitted = jnp.sum(picked * work[SOURCE_SPREAD, at], axis=0, keepdims=True)
        cleaned = work[IMAGE, at] - fitted
        total = total + dot_nt(split_rows(work[KNOT_SPREAD, at] * cleaned), hot_rows(knot_numbers, work[KNOT_LANE, at]))
    return join_rows(total)


def with_ends(total, earlier, later, energy):
    lane = lax.broadcasted_iota(jnp.int32, (16, 256), 1)
    within = lax.broadcasted_iota(jnp.int32, (16, 256), 0) < 12
    beyond = jnp.where(within, total[64:80], 0.0)
    low = total[0:16] + jnp.where(lane == 0, jnp.where(within, earlier, 0.0), pltpu.roll(beyond, 1, 1))
    after_end = beyond[:, 255:256] + jnp.where(lax.broadcasted_iota(jnp.int32, (16, 1), 0) < 12, later, 0.0)
    lane = lax.broadcasted_iota(jnp.int32, (8, 128), 1)
    beside = jnp.where(lane == 0, after_end[0:8], jnp.where(lane == 1, after_end[8:16], 0.0))
    return jnp.concatenate([low, total[16:64], jnp.concatenate([energy, beside], axis=1)], axis=0)


def first_kernel(tm_ref, own, one, three, two, twin, _work, _state, knots_ref, work, state):
    sums = (own[0:160] + two[...]) + (one[0:160] + three[0:160])
    odd = (tm_ref[0] & 1) == 1
    earlier = jnp.where(odd, twin[...], one[160:192])
    later = jnp.where(odd, three[160:192], twin[...])
    factor = factorize(factor_of(sums))
    stacked = jnp.concatenate([factor[pair] for pair in entry_pairs], axis=0)
    put(state, FACTOR_A, 0, stacked[0:80])
    put(state, FACTOR_B, 0, stacked[80:120])
    put(state, FACTOR_B, 40, sums[120:160])
    ghosts = unpacked(jnp.concatenate([earlier[0:16], earlier[16:32], later[0:16], later[16:32]], axis=1))
    put_ghosts(state, ghosts)
    solved = split_rows(jnp.concatenate(chol_solve(factor, [tile(sums, 15 + j) for j in range(5)]), axis=0))
    earlier, later = ghost_sums(solved, ghosts, ghosts[22:23])
    knots_ref[...] = with_ends(eliminate_and_spread(solved, work), earlier, later, jnp.zeros((8, 128), f32))


def kept_factor(state):
    return factor_of(jnp.concatenate([get(state, FACTOR_A, 0, 80), get(state, FACTOR_B, 0, 40)], axis=0))


def back(lanes, at_tm, parts, work, state):
    sums = four(parts)
    put(state, lanes, 0, sums[:-8])
    target = [tile(sums, j) for j in range(5)]
    solved = chol_solve(kept_factor(state), target)
    energy = jnp.where(lax.broadcasted_iota(jnp.int32, (8, 128), 0) == 0, tile(sums, 5), 0.0)
    for j in range(5):
        energy = energy - target[j] * solved[j]
    solved = split_rows(jnp.concatenate(solved, axis=0))
    ends = zip(ghost_sums(solved, get_ghosts(state), 0.0), end_parts(at_tm, sums[-8:]))
    earlier, later = (ghost + image for ghost, image in ends)
    return with_ends(eliminate_and_spread(solved, work), earlier, later, energy), energy


def back_kernel(tm_ref, own, one, three, two, _work, _state, knots_ref, work, state):
    knots_ref[...], _ = back(BEFORE, tm_ref[0], (own, one, three, two), work, state)


def back_to_owners_kernel(tm_ref, own, one, three, two, _work, _state, blocks_ref, work, state):
    knots, energy = back(AFTER, tm_ref[0], (own, one, three, two), work, state)
    group = lax.broadcasted_iota(jnp.int32, (8, 128), 1) >> 4
    for half in range(2):
        tiles = [knots[8 * q : 8 * q + 8, 128 * half : 128 * half + 128] for q in range(8)]
        for stage in (1, 2, 4):
            at_first = (group & stage) == 0
            for q in range(8):
                if q & stage == 0:
                    here, there = tiles[q], tiles[q + stage]
                    tiles[q] = jnp.where(at_first, here, pltpu.roll(there, 16 * stage, 1))
                    tiles[q + stage] = jnp.where(at_first, pltpu.roll(here, 128 - 16 * stage, 1), there)
        for at in range(8):
            blocks_ref[8 * half + at, 0:8] = tiles[at]
            blocks_ref[8 * half + at, 8:16] = energy


def assembled(knots):
    lane = lax.broadcasted_iota(jnp.int32, (16, 256), 1)
    row = lax.broadcasted_iota(jnp.int32, (16, 256), 0)
    after_end = jnp.concatenate([knots[64:72, 128:129], knots[64:72, 129:130]], axis=0)
    following = jnp.where(lane == 255, after_end, pltpu.roll(knots[0:16], 255, 1))
    return jnp.concatenate([knots[0:64], jnp.where(row < 12, following, 0.0)], axis=0)


def energy_of(knots):
    return jnp.sum(knots[64:72, 0:128])


def folded(left, right):
    product = left[0:64] * right[0:64]
    return jnp.sum(product[:, 0:128] + product[:, 128:256], axis=0, keepdims=True)


def lane_blocks(value):
    return functools.reduce(jnp.add, [value[:, start : start + 128] for start in range(0, CHUNK, 128)])


def gather_and_sum(at_tm, field, work):
    source_numbers, knot_numbers = row_numbers(128), row_numbers(256)
    parts = split_rows(field)
    total = jnp.zeros((120, 128), f32)
    square = jnp.zeros((1, 128), f32)
    high = jnp.zeros((16, 128), f32)
    low = jnp.zeros((16, 128), f32)
    for at in chunks():
        knot_lane = work[KNOT_LANE, at]
        picked = join_rows(dot_nn(parts, hot_rows(knot_numbers, knot_lane)))
        image = jnp.sum(picked * work[KNOT_SPREAD, at], axis=0, keepdims=True)
        work[IMAGE, at] = image
        square = square + lane_blocks(image * image)
        high = high + lane_blocks(work[104:120, at] * jnp.where(knot_lane == 255.0, image, 0.0))
        low = low + lane_blocks(work[40:56, at] * jnp.where(knot_lane == 0.0, image, 0.0))
        total = total + dot_nt(split_rows(work[SOURCE_SPREAD, at] * image), hot_rows(source_numbers, work[SOURCE_LANE, at]))
    ends = end_tile(at_tm, jnp.sum(high, axis=1, keepdims=True), jnp.sum(low, axis=1, keepdims=True))
    return join_rows(total), square, ends


def start_kernel(tm_ref, own, one, three, two, _work, _state, sums_ref, work, state):
    residual = assembled(four((own, one, three, two)))
    put(state, START, 0, residual)
    sums, square, ends = gather_and_sum(tm_ref[0], residual, work)
    norm = folded(residual, residual)
    sums_ref[...] = jnp.concatenate([sums, square, norm, jnp.zeros((6, 128), f32), ends], axis=0)


def next_kernel(tm_ref, own, one, three, two, _work, _state, sums_ref, work, state):
    knots = four((own, one, three, two))
    direction = get(state, START, 0, 80)
    mapped = assembled(knots) + damping * direction
    norm_now = jnp.sum(get(state, BEFORE, 41, 1))
    product = energy_of(knots) + damping * norm_now
    residual = direction - (norm_now / product) * mapped
    put(state, MAPPED, 0, mapped)
    put(state, RESIDUAL, 0, residual)
    put(state, SCALAR, 0, jnp.zeros((8, 128), f32) + product)
    sums, square, ends = gather_and_sum(tm_ref[0], residual, work)
    norm, crossed = folded(residual, residual), folded(residual, mapped)
    sums_ref[...] = jnp.concatenate([sums, square, norm, crossed, jnp.zeros((5, 128), f32), ends], axis=0)


OWN = ((152, 128), f32)


def own_kernel(place_ref, state, own_ref):
    place = place_ref[0]
    lane_place = lax.broadcasted_iota(jnp.int32, (8, 128), 1) >> 4
    for at, lanes in enumerate((START, MAPPED, RESIDUAL)):
        result = jnp.zeros((8, 128), f32)
        for q in range(8):
            rows = get(state, lanes, 8 * q, 8)
            rows = jnp.where(place >= 8, rows[:, 128:256], rows[:, 0:128])
            rows = pltpu.roll(rows, (16 * (q - place)) & 127, 1)
            result = jnp.where(lane_place == q, rows, result)
        own_ref[8 * at : 8 * at + 8] = result
    factor = kept_factor(state)
    for at, value in enumerate((get(state, FACTOR_B, 40, 40), get(state, BEFORE, 0, 40), get(state, AFTER, 0, 40))):
        start = 24 + 40 * at
        own_ref[start : start + 40] = jnp.concatenate(chol_solve(factor, [tile(value, j) for j in range(5)]), axis=0)
    norm_first = jnp.sum(get(state, BEFORE, 41, 1))
    norm_now = jnp.sum(get(state, AFTER, 41, 1))
    crossed = jnp.sum(get(state, AFTER, 42, 1))
    product_first = jnp.max(get(state, SCALAR, 0, 8))
    alpha_first = norm_first / product_first
    beta = norm_now / norm_first
    product = damping * norm_now + beta * (2.0 * crossed + beta * product_first)
    row = lax.broadcasted_iota(jnp.int32, (8, 128), 0)
    scalars = jnp.zeros((8, 128), f32)
    for at, value in enumerate((alpha_first, beta, norm_now, product)):
        scalars = jnp.where(row == at, value, scalars)
    own_ref[144:152] = scalars


def last_kernel(blocks_ref, own_ref, solution_ref, left_ref, source_ref):
    blocks = functools.reduce(jnp.add, [blocks_ref[at] for at in range(16)])
    start, mapped, residual = own_ref[0:8], own_ref[8:16], own_ref[16:24]
    alpha_first, beta, norm_now, product = (own_ref[144 + at : 145 + at] for at in range(4))
    alpha = norm_now / (jnp.sum(blocks[8:16]) + product)
    from_start = alpha_first + alpha * beta
    image = blocks[0:8] + damping * residual
    solution = from_start * start + alpha * residual
    left = residual - alpha * (image + beta * mapped)
    both = split_rows(jnp.concatenate([solution, left], axis=0))
    held = lax.broadcasted_iota(jnp.int32, (128, 256), 0)
    wanted = lax.broadcasted_iota(jnp.int32, (128, 256), 1)
    same = (held & 15) == (wanted >> 4)
    halves = [
        join_rows(dot_nn(both, jnp.where(same & ((wanted & 15) == 2 * (held >> 4) + upper), 1.0, 0.0).astype(bf16)))
        for upper in range(2)
    ]
    for at, ref in enumerate((solution_ref, left_ref)):
        own_rows = halves[0][8 * at : 8 * at + 4] + halves[1][8 * at + 4 : 8 * at + 8]
        for c in range(4):
            ref[c] = own_rows[c : c + 1]
    for j in range(5):
        plain, before, after = (own_ref[start + 8 * j : start + 8 * j + 8] for start in (24, 64, 104))
        solved = plain - from_start * before - alpha * after
        for a in range(8):
            source_ref[j : j + 1, 128 * a : 128 * a + 128] = solved[a : a + 1]


VMEM = pl.BlockSpec(memory_space=pltpu.VMEM)
SMEM = pl.BlockSpec(memory_space=pltpu.SMEM)


def call(kernel, name, outs, *operands, scalars=0, aliases=None, work_ahead=0):
    specs = [SMEM] * scalars + [VMEM] * (len(operands) - scalars)
    shapes = [jax.ShapeDtypeStruct(shape, dtype) for shape, dtype in outs]
    return pl.pallas_call(
        kernel,
        out_shape=shapes,
        in_specs=specs,
        out_specs=[VMEM] * len(outs),
        input_output_aliases=aliases or {},
        compiler_params=pltpu.CompilerParams(vmem_limit_bytes=8 * 1024 * 1024),
        cost_estimate=pl.CostEstimate(flops=work_ahead, bytes_accessed=0, transcendentals=0) if work_ahead else None,
        name=name,
    )(*operands)


def ring_parts(value, axis):
    count = lax.axis_size(axis)
    return [value] + [
        lax.ppermute(value, axis, [(at, (at + step) % count) for at in range(count)]) for step in (1, 3, 2)
    ]


def crossing(value, step):
    chips = lax.axis_size("tm_0")
    pairs = [(2 * at + core, 2 * ((at + step) % chips) + 1 - core) for at in range(chips) for core in range(2)]
    return lax.ppermute(value, TM, pairs)


def to_twin(value):
    return lax.ppermute(value, "tm_1", [(0, 1), (1, 0)])


def tm_parts(value):
    value = value + to_twin(value)
    return ring_parts(value, "tm_0")


def sky_parts(knots):
    own, one, three, two = ring_parts(knots, "sky_1")
    return ring_parts((one + three) + (two + own), "sky_0")


KNOTS = ((72, 256), f32)
GHOSTS = ((32, 128), f32)
SUMS = ((56, 128), f32)


def shards(obs_source, obs_knot, obs_count, src_design, att_design, obs_phase, obs_value, src_prior):
    at = lax.axis_index(TM)
    first = (at == 0).astype(jnp.int32).reshape(1)
    last = (at == lax.axis_size(TM) - 1).astype(jnp.int32).reshape(1)
    tm = at.astype(jnp.int32).reshape(1)
    place = lax.axis_index(SKY).astype(jnp.int32).reshape(1)
    line = lambda value: value.reshape(1, OBS_DEV)
    (state,) = call(open_kernel, "open", [STATE], work_ahead=1 << 32)
    work, sums, state = call(
        source_kernel,
        "source_sums",
        [WORK, ((160, 128), f32), STATE],
        obs_count, first, line(obs_source), src_design, line(obs_value), src_prior, state,
        aliases={6: 2},
        scalars=2,
    )
    twin_sums = to_twin(sums)
    earlier, later, twin = call(
        ghost_kernel,
        "ghosts",
        [GHOSTS] * 3,
        obs_count, tm, obs_knot.reshape(32, 128), line(obs_knot), line(obs_source), src_design, att_design, line(obs_phase), work,
        scalars=2,
    )
    sums = sums + twin_sums
    onward = jnp.concatenate([sums, later], axis=0)
    parts = (
        onward,
        crossing(onward, 1),
        crossing(jnp.concatenate([sums, earlier], axis=0), -1),
        lax.ppermute(sums, "tm_0", [(at, (at + 2) % 4) for at in range(4)]),
        to_twin(twin),
    )
    (work,) = call(
        knot_kernel,
        "knot_spread",
        [WORK],
        obs_count, last, line(obs_knot), att_design, line(obs_phase), work,
        scalars=2,
        aliases={5: 0},
    )
    knots, work, state = call(
        first_kernel, "first", [KNOTS, WORK, STATE], tm, *parts, work, state, scalars=1, aliases={6: 1, 7: 2}
    )
    parts = sky_parts(knots)
    kept = dict(scalars=1, aliases={5: 1, 6: 2})
    sums, work, state = call(start_kernel, "start", [SUMS, WORK, STATE], tm, *parts, work, state, **kept)
    parts = tm_parts(sums)
    knots, work, state = call(back_kernel, "back", [KNOTS, WORK, STATE], tm, *parts, work, state, **kept)
    parts = sky_parts(knots)
    sums, work, state = call(next_kernel, "next", [SUMS, WORK, STATE], tm, *parts, work, state, **kept)
    parts = tm_parts(sums)
    blocks, work, state = call(
        back_to_owners_kernel, "back_to_owners", [((16, 16, 128), f32), WORK, STATE], tm, *parts, work, state, **kept
    )
    (own,) = call(own_kernel, "own", [OWN], place, state, scalars=1)
    blocks = lax.all_to_all(blocks, SKY, 0, 0, tiled=True)
    return call(
        last_kernel,
        "last",
        [((4, 1, 256), f32), ((4, 1, 256), f32), ((5, 1024), f32)],
        blocks, own,
    )


def solution(mesh):
    torus = Mesh(mesh.devices.reshape(4, 4, 4, 2), SKY_TM)
    placed = (
        P(SKY_TM),
        P(SKY_TM),
        P(SKY_TM),
        P(None, SKY_TM),
        P(None, SKY_TM),
        P(SKY_TM),
        P(SKY_TM),
        P(None, SKY),
    )
    return jax.shard_map(
        shards,
        mesh=torus,
        in_specs=placed,
        out_specs=(P(None, TM, SKY), P(None, TM, SKY), P(None, SKY)),
        check_vma=False,
    )
```

```python
import functools

import jax
import jax.numpy as jnp
from jax import lax
from jax.experimental import pallas as pl
from jax.experimental.pallas import tpu as pltpu
from jax.sharding import Mesh
from jax.sharding import PartitionSpec as P

SKY = ("sky_0", "sky_1")
TM = ("tm_0", "tm_1")
SKY_TM = ("sky_0", "sky_1", "tm_0", "tm_1")

OBS_DEV = 4096
SEGMENTS = 8
CHUNK = 4096
damping = 0.5
entry_pairs = [(row_at, col_at) for row_at in range(5) for col_at in range(row_at + 1)]


f32 = jnp.float32
bf16 = jnp.bfloat16


def split_rows(value):
    first = value.astype(bf16)
    rest = value - first.astype(f32)
    second = rest.astype(bf16)
    third = (rest - second.astype(f32)).astype(bf16)
    return jnp.concatenate([first, second, third], axis=0)


def join_rows(stacked):
    rows = stacked.shape[0] // 3
    return stacked[:rows] + (stacked[rows : 2 * rows] + stacked[2 * rows :])


def dot_nt(left, right):
    return lax.dot_general(left, right, (((1,), (1,)), ((), ())), preferred_element_type=f32)


def dot_nn(left, right):
    return lax.dot_general(left, right, (((1,), (0,)), ((), ())), preferred_element_type=f32)


def chunks():
    return [slice(start, start + CHUNK) for start in range(0, OBS_DEV, CHUNK)]


def four(refs):
    own, one, three, two = (ref[...] for ref in refs)
    return (own + two) + (one + three)


def lanes_from(start, rows):
    return lax.broadcasted_iota(jnp.int32, (rows, CHUNK), 1) + start


SOURCE_SPREAD = slice(0, 40)
KNOT_SPREAD = slice(40, 120)
IMAGE = slice(120, 121)
SOURCE_LANE = slice(121, 122)
KNOT_LANE = slice(122, 123)
START, MAPPED, RESIDUAL = (slice(at, at + 256) for at in (0, 256, 512))
FACTOR_A, FACTOR_B, BEFORE, AFTER, SCALAR = (slice(at, at + 128) for at in (768, 896, 1024, 1152, 1280))
WORK = ((128, OBS_DEV), f32)
STATE = ((80, 1408), f32)


def put(state, lanes, start, value):
    state[start : start + value.shape[0], lanes] = value


def get(state, lanes, start, rows):
    return state[start : start + rows, lanes]


GHOST_PLACES = ((SCALAR, 8), (SCALAR, 32), (SCALAR, 56), (BEFORE, 56))


def put_ghosts(state, ghosts):
    for at, (lanes, start) in enumerate(GHOST_PLACES):
        put(state, lanes, start, ghosts[:, 128 * at : 128 * at + 128])


def get_ghosts(state):
    return jnp.concatenate([get(state, lanes, start, 24) for lanes, start in GHOST_PLACES], axis=1)


def row_numbers(rows, lanes=CHUNK):
    return lax.broadcasted_iota(jnp.int32, (rows, lanes), 0).astype(f32).astype(bf16)


def hot_rows(numbers, lane_row):
    wanted = jnp.broadcast_to(lane_row, numbers.shape).astype(bf16)
    return jnp.where(numbers == wanted, jnp.ones_like(numbers), jnp.zeros_like(numbers))


def open_kernel(state):
    state[0:8, 0:128] = jnp.zeros((8, 128), f32)


def source_kernel(count_ref, first_ref, source_ref, g_ref, y_ref, prior_ref, _state, work, sums_ref, state):
    numbers = row_numbers(128)
    total = jnp.zeros((480, 128), f32)
    for at in chunks():
        live = lanes_from(at.start, 1) < count_ref[0]
        source = source_ref[:, at]
        lane = (source & 127).astype(f32)
        work[SOURCE_LANE, at] = lane
        mark = jnp.where(live, source >> 7, -1)
        chosen = jnp.where(lax.broadcasted_iota(jnp.int32, (8, CHUNK), 0) == mark, 1.0, 0.0)
        g = [g_ref[j : j + 1, at] for j in range(5)]
        y = y_ref[:, at]
        work[IMAGE, at] = y
        spread = [chosen * g[j] for j in range(5)]
        for j in range(5):
            work[8 * j : 8 * j + 8, at] = spread[j]
        rows = [spread[r] * g[c] for r, c in entry_pairs] + [spread[j] * y for j in range(5)]
        total = total + dot_nt(split_rows(jnp.concatenate(rows, axis=0)), hot_rows(numbers, lane))
    sums_ref[...] = join_rows(total)
    once = jnp.where(first_ref[0] == 1, 1.0, 0.0)
    for at, (row_at, col_at) in enumerate(entry_pairs):
        if row_at == col_at:
            prior = jnp.concatenate([prior_ref[row_at : row_at + 1, 128 * a : 128 * a + 128] for a in range(8)], axis=0)
            sums_ref[8 * at : 8 * at + 8] += prior * once


def spline_taps(phase):
    squared = phase * phase
    cubed = squared * phase
    rest = 1.0 - phase
    return (
        rest * rest * rest / 6.0,
        (3.0 * cubed - 6.0 * squared + 4.0) / 6.0,
        (-3.0 * cubed + 3.0 * squared + 3.0 * phase + 1.0) / 6.0,
        cubed / 6.0,
    )


def tap_at(taps, gap):
    weight = jnp.where(gap == 0, taps[0], 0.0)
    for m in range(1, 4):
        weight = jnp.where(gap == m, taps[m], weight)
    return weight


def knot_kernel(count_ref, last_ref, knot_ref, h_ref, phase_ref, _work, work):
    upper = lax.broadcasted_iota(jnp.int32, (8, CHUNK), 0) >> 2
    for at in chunks():
        live = lanes_from(at.start, 1) < count_ref[0]
        knot = knot_ref[:, at]
        high = knot >> 4
        work[KNOT_LANE, at] = high.astype(f32)
        h = jnp.where(live, h_ref[:, at], 0.0)
        h = jnp.concatenate([h, h], axis=0)
        taps = [jnp.broadcast_to(tap, (8, CHUNK)) for tap in spline_taps(phase_ref[:, at])]
        ahead = upper - (knot & 15)
        kept = jnp.where((high == 255) & (last_ref[0] == 1), 0.0, 1.0)
        for q in range(10):
            weight = tap_at(taps, ahead + 2 * q)
            if q >= 8:
                weight = weight * kept
            row = KNOT_SPREAD.start + 8 * q
            work[row : row + 8, at] = weight * h


def ghost_kernel(count_ref, tm_ref, flat_ref, knot_ref, source_ref, g_ref, h_ref, phase_ref, work, earlier_ref, later_ref, twin_ref):
    knot = flat_ref[...]
    order = lax.broadcasted_iota(jnp.int32, (32, 128), 0) * 128 + lax.broadcasted_iota(jnp.int32, (32, 128), 1)
    live = order < count_ref[0]
    across = jnp.where(
        lax.broadcasted_iota(jnp.int32, (128, 128), 0) < lax.broadcasted_iota(jnp.int32, (128, 128), 1), 1.0, 0.0
    ).astype(bf16)
    down = jnp.where(
        lax.broadcasted_iota(jnp.int32, (32, 32), 0) > lax.broadcasted_iota(jnp.int32, (32, 32), 1), 1.0, 0.0
    ).astype(bf16)
    numbers = row_numbers(256, 128)
    at_low = live & (knot < 3) & (tm_ref[0] > 0)
    at_high = live & (knot >= 4093) & (tm_ref[0] < SEGMENTS - 1)
    totals = []
    for chosen, origin in ((at_high, 4096), (at_low, 0)):
        mark = jnp.where(chosen, 1.0, 0.0).astype(bf16)
        rank = dot_nn(mark, across) + jnp.sum(dot_nn(down, mark), axis=1, keepdims=True)
        rank = jnp.where(chosen, rank, -1.0)
        total = jnp.zeros((48, 256), f32)
        for at in chunks():
            first = at.start // 128
            slots = jnp.concatenate([hot_rows(numbers, rank[row : row + 1]) for row in range(first, first + CHUNK // 128)], axis=1)
            place = (knot_ref[:, at] - origin).astype(f32)
            data = jnp.concatenate(
                [g_ref[:, at], source_ref[:, at].astype(f32), work[IMAGE, at], phase_ref[:, at], place, h_ref[:, at], jnp.zeros((3, CHUNK), f32)],
                axis=0,
            )
            total = total + dot_nt(split_rows(data), slots)
        totals.append(join_rows(total))
    for total, ref in zip(totals, (later_ref, earlier_ref)):
        ref[0:16] = total[:, 0:128]
        ref[16:32] = total[:, 128:256]
    twin_ref[...] = jnp.where((tm_ref[0] & 1) == 1, earlier_ref[...], later_ref[...])


def unpacked(packed):
    taps = [jnp.broadcast_to(tap, (16, 512)) for tap in spline_taps(packed[7:8])]
    row = lax.broadcasted_iota(jnp.int32, (16, 512), 0)
    weight = tap_at(taps, (row >> 2) - packed[8:9].astype(jnp.int32))
    h = jnp.concatenate([packed[9:13]] * 4, axis=0)
    return jnp.concatenate([weight * h, packed[0:7], jnp.zeros((1, 512), f32)], axis=0)


def ghost_sums(solved, ghosts, values):
    source = ghosts[21:22].astype(jnp.int32)
    picked = join_rows(dot_nn(solved, hot_rows(row_numbers(128, 512), (source & 127).astype(f32))))
    fitted = functools.reduce(jnp.add, [tile(picked, j) * ghosts[16 + j : 17 + j] for j in range(5)])
    fitted = jnp.where(lax.broadcasted_iota(jnp.int32, (8, 512), 0) == (source >> 7), fitted, 0.0)
    weighted = ghosts[0:16] * (values - jnp.sum(fitted, axis=0, keepdims=True))
    return jnp.sum(weighted[:, 0:256], axis=1, keepdims=True), jnp.sum(weighted[:, 256:512], axis=1, keepdims=True)


def end_tile(at_tm, high, low):
    lane = lax.broadcasted_iota(jnp.int32, (8, 128), 1)
    result = jnp.zeros((8, 128), f32)
    for place, part in enumerate((high[0:8], high[8:16], low[0:8], low[8:16])):
        result = jnp.where(lane == at_tm + 16 * place, part, result)
    return result


def end_parts(at_tm, ends):
    lane = lax.broadcasted_iota(jnp.int32, (8, 128), 1)
    pick = lambda at: jnp.sum(jnp.where(lane == at, ends, 0.0), axis=1, keepdims=True)
    earlier = jnp.concatenate([pick(at_tm - 1), pick(at_tm + 15)], axis=0)
    later = jnp.concatenate([pick(at_tm + 33), pick(at_tm + 49)], axis=0)
    return earlier, later


def tile(value, at):
    return value[8 * at : 8 * at + 8]


def factor_of(value):
    return {pair: tile(value, at) for at, pair in enumerate(entry_pairs)}


def factorize(normal):
    factor = {}
    for row_at in range(5):
        for col_at in range(row_at + 1):
            running = normal[row_at, col_at]
            for inner_at in range(col_at):
                running = running - factor[row_at, inner_at] * factor[col_at, inner_at]
            if row_at == col_at:
                factor[row_at, row_at] = 1.0 / jnp.sqrt(running)
            else:
                factor[row_at, col_at] = running * factor[col_at, col_at]
    return factor


def chol_solve(factor, target):
    forward = []
    for row_at in range(5):
        running = target[row_at]
        for inner_at in range(row_at):
            running = running - factor[row_at, inner_at] * forward[inner_at]
        forward.append(running * factor[row_at, row_at])
    result = [None] * 5
    for row_at in reversed(range(5)):
        running = forward[row_at]
        for inner_at in range(row_at + 1, 5):
            running = running - factor[inner_at, row_at] * result[inner_at]
        result[row_at] = running * factor[row_at, row_at]
    return result


def eliminate_and_spread(solved, work):
    source_numbers, knot_numbers = row_numbers(128), row_numbers(256)
    total = jnp.zeros((240, 256), f32)
    for at in chunks():
        picked = join_rows(dot_nn(solved, hot_rows(source_numbers, work[SOURCE_LANE, at])))
        fitted = jnp.sum(picked * work[SOURCE_SPREAD, at], axis=0, keepdims=True)
        cleaned = work[IMAGE, at] - fitted
        total = total + dot_nt(split_rows(work[KNOT_SPREAD, at] * cleaned), hot_rows(knot_numbers, work[KNOT_LANE, at]))
    return join_rows(total)


def with_ends(total, earlier, later, energy):
    lane = lax.broadcasted_iota(jnp.int32, (16, 256), 1)
    within = lax.broadcasted_iota(jnp.int32, (16, 256), 0) < 12
    beyond = jnp.where(within, total[64:80], 0.0)
    low = total[0:16] + jnp.where(lane == 0, jnp.where(within, earlier, 0.0), pltpu.roll(beyond, 1, 1))
    after_end = beyond[:, 255:256] + jnp.where(lax.broadcasted_iota(jnp.int32, (16, 1), 0) < 12, later, 0.0)
    lane = lax.broadcasted_iota(jnp.int32, (8, 128), 1)
    beside = jnp.where(lane == 0, after_end[0:8], jnp.where(lane == 1, after_end[8:16], 0.0))
    return jnp.concatenate([low, total[16:64], jnp.concatenate([energy, beside], axis=1)], axis=0)


def first_kernel(tm_ref, own, one, three, two, twin, _work, _state, knots_ref, work, state):
    sums = (own[0:160] + two[...]) + (one[0:160] + three[0:160])
    odd = (tm_ref[0] & 1) == 1
    earlier = jnp.where(odd, twin[...], one[160:192])
    later = jnp.where(odd, three[160:192], twin[...])
    factor = factorize(factor_of(sums))
    stacked = jnp.concatenate([factor[pair] for pair in entry_pairs], axis=0)
    put(state, FACTOR_A, 0, stacked[0:80])
    put(state, FACTOR_B, 0, stacked[80:120])
    put(state, FACTOR_B, 40, sums[120:160])
    ghosts = unpacked(jnp.concatenate([earlier[0:16], earlier[16:32], later[0:16], later[16:32]], axis=1))
    put_ghosts(state, ghosts)
    solved = split_rows(jnp.concatenate(chol_solve(factor, [tile(sums, 15 + j) for j in range(5)]), axis=0))
    earlier, later = ghost_sums(solved, ghosts, ghosts[22:23])
    knots_ref[...] = with_ends(eliminate_and_spread(solved, work), earlier, later, jnp.zeros((8, 128), f32))


def kept_factor(state):
    return factor_of(jnp.concatenate([get(state, FACTOR_A, 0, 80), get(state, FACTOR_B, 0, 40)], axis=0))


def back(lanes, at_tm, parts, work, state):
    sums = four(parts)
    put(state, lanes, 0, sums[:-8])
    target = [tile(sums, j) for j in range(5)]
    solved = chol_solve(kept_factor(state), target)
    energy = jnp.where(lax.broadcasted_iota(jnp.int32, (8, 128), 0) == 0, tile(sums, 5), 0.0)
    for j in range(5):
        energy = energy - target[j] * solved[j]
    solved = split_rows(jnp.concatenate(solved, axis=0))
    ends = zip(ghost_sums(solved, get_ghosts(state), 0.0), end_parts(at_tm, sums[-8:]))
    earlier, later = (ghost + image for ghost, image in ends)
    return with_ends(eliminate_and_spread(solved, work), earlier, later, energy), energy


def back_kernel(tm_ref, own, one, three, two, _work, _state, knots_ref, work, state):
    knots_ref[...], _ = back(BEFORE, tm_ref[0], (own, one, three, two), work, state)


def back_to_owners_kernel(tm_ref, place_ref, own, one, three, two, _work, _state, blocks_ref, own_ref, work, state):
    knots, energy = back(AFTER, tm_ref[0], (own, one, three, two), work, state)
    group = lax.broadcasted_iota(jnp.int32, (8, 128), 1) >> 4
    for half in range(2):
        tiles = [knots[8 * q : 8 * q + 8, 128 * half : 128 * half + 128] for q in range(8)]
        for stage in (1, 2, 4):
            at_first = (group & stage) == 0
            for q in range(8):
                if q & stage == 0:
                    here, there = tiles[q], tiles[q + stage]
                    tiles[q] = jnp.where(at_first, here, pltpu.roll(there, 16 * stage, 1))
                    tiles[q + stage] = jnp.where(at_first, pltpu.roll(here, 128 - 16 * stage, 1), there)
        for at in range(8):
            blocks_ref[8 * half + at, 0:8] = tiles[at]
            blocks_ref[8 * half + at, 8:16] = energy
    put_own(place_ref[0], state, own_ref)


def assembled(knots):
    lane = lax.broadcasted_iota(jnp.int32, (16, 256), 1)
    row = lax.broadcasted_iota(jnp.int32, (16, 256), 0)
    after_end = jnp.concatenate([knots[64:72, 128:129], knots[64:72, 129:130]], axis=0)
    following = jnp.where(lane == 255, after_end, pltpu.roll(knots[0:16], 255, 1))
    return jnp.concatenate([knots[0:64], jnp.where(row < 12, following, 0.0)], axis=0)


def energy_of(knots):
    return jnp.sum(knots[64:72, 0:128])


def folded(left, right):
    product = left[0:64] * right[0:64]
    return jnp.sum(product[:, 0:128] + product[:, 128:256], axis=0, keepdims=True)


def lane_blocks(value):
    return functools.reduce(jnp.add, [value[:, start : start + 128] for start in range(0, CHUNK, 128)])


def gather_and_sum(at_tm, field, work):
    source_numbers, knot_numbers = row_numbers(128), row_numbers(256)
    parts = split_rows(field)
    total = jnp.zeros((120, 128), f32)
    square = jnp.zeros((1, 128), f32)
    high = jnp.zeros((16, 128), f32)
    low = jnp.zeros((16, 128), f32)
    for at in chunks():
        knot_lane = work[KNOT_LANE, at]
        picked = join_rows(dot_nn(parts, hot_rows(knot_numbers, knot_lane)))
        image = jnp.sum(picked * work[KNOT_SPREAD, at], axis=0, keepdims=True)
        work[IMAGE, at] = image
        square = square + lane_blocks(image * image)
        high = high + lane_blocks(work[104:120, at] * jnp.where(knot_lane == 255.0, image, 0.0))
        low = low + lane_blocks(work[40:56, at] * jnp.where(knot_lane == 0.0, image, 0.0))
        total = total + dot_nt(split_rows(work[SOURCE_SPREAD, at] * image), hot_rows(source_numbers, work[SOURCE_LANE, at]))
    ends = end_tile(at_tm, jnp.sum(high, axis=1, keepdims=True), jnp.sum(low, axis=1, keepdims=True))
    return join_rows(total), square, ends


def start_kernel(tm_ref, own, one, three, two, _work, _state, sums_ref, work, state):
    residual = assembled(four((own, one, three, two)))
    put(state, START, 0, residual)
    sums, square, ends = gather_and_sum(tm_ref[0], residual, work)
    norm = folded(residual, residual)
    sums_ref[...] = jnp.concatenate([sums, square, norm, jnp.zeros((6, 128), f32), ends], axis=0)


def next_kernel(tm_ref, own, one, three, two, _work, _state, sums_ref, work, state):
    knots = four((own, one, three, two))
    direction = get(state, START, 0, 80)
    mapped = assembled(knots) + damping * direction
    norm_now = jnp.sum(get(state, BEFORE, 41, 1))
    product = energy_of(knots) + damping * norm_now
    residual = direction - (norm_now / product) * mapped
    put(state, MAPPED, 0, mapped)
    put(state, RESIDUAL, 0, residual)
    put(state, SCALAR, 0, jnp.zeros((8, 128), f32) + product)
    sums, square, ends = gather_and_sum(tm_ref[0], residual, work)
    norm, crossed = folded(residual, residual), folded(residual, mapped)
    sums_ref[...] = jnp.concatenate([sums, square, norm, crossed, jnp.zeros((5, 128), f32), ends], axis=0)


OWN = ((152, 128), f32)


def put_own(place, state, own_ref):
    lane_place = lax.broadcasted_iota(jnp.int32, (8, 128), 1) >> 4
    for at, lanes in enumerate((START, MAPPED, RESIDUAL)):
        result = jnp.zeros((8, 128), f32)
        for q in range(8):
            rows = get(state, lanes, 8 * q, 8)
            rows = jnp.where(place >= 8, rows[:, 128:256], rows[:, 0:128])
            rows = pltpu.roll(rows, (16 * (q - place)) & 127, 1)
            result = jnp.where(lane_place == q, rows, result)
        own_ref[8 * at : 8 * at + 8] = result
    factor = kept_factor(state)
    for at, value in enumerate((get(state, FACTOR_B, 40, 40), get(state, BEFORE, 0, 40), get(state, AFTER, 0, 40))):
        start = 24 + 40 * at
        own_ref[start : start + 40] = jnp.concatenate(chol_solve(factor, [tile(value, j) for j in range(5)]), axis=0)
    norm_first = jnp.sum(get(state, BEFORE, 41, 1))
    norm_now = jnp.sum(get(state, AFTER, 41, 1))
    crossed = jnp.sum(get(state, AFTER, 42, 1))
    product_first = jnp.max(get(state, SCALAR, 0, 8))
    alpha_first = norm_first / product_first
    beta = norm_now / norm_first
    product = damping * norm_now + beta * (2.0 * crossed + beta * product_first)
    row = lax.broadcasted_iota(jnp.int32, (8, 128), 0)
    scalars = jnp.zeros((8, 128), f32)
    for at, value in enumerate((alpha_first, beta, norm_now, product)):
        scalars = jnp.where(row == at, value, scalars)
    own_ref[144:152] = scalars


def last_kernel(blocks_ref, own_ref, solution_ref, left_ref, source_ref):
    blocks = functools.reduce(jnp.add, [blocks_ref[at] for at in range(16)])
    start, mapped, residual = own_ref[0:8], own_ref[8:16], own_ref[16:24]
    alpha_first, beta, norm_now, product = (own_ref[144 + at : 145 + at] for at in range(4))
    alpha = norm_now / (jnp.sum(blocks[8:16]) + product)
    from_start = alpha_first + alpha * beta
    image = blocks[0:8] + damping * residual
    solution = from_start * start + alpha * residual
    left = residual - alpha * (image + beta * mapped)
    both = split_rows(jnp.concatenate([solution, left], axis=0))
    held = lax.broadcasted_iota(jnp.int32, (128, 256), 0)
    wanted = lax.broadcasted_iota(jnp.int32, (128, 256), 1)
    same = (held & 15) == (wanted >> 4)
    halves = [
        join_rows(dot_nn(both, jnp.where(same & ((wanted & 15) == 2 * (held >> 4) + upper), 1.0, 0.0).astype(bf16)))
        for upper in range(2)
    ]
    for at, ref in enumerate((solution_ref, left_ref)):
        own_rows = halves[0][8 * at : 8 * at + 4] + halves[1][8 * at + 4 : 8 * at + 8]
        for c in range(4):
            ref[c] = own_rows[c : c + 1]
    for j in range(5):
        plain, before, after = (own_ref[start + 8 * j : start + 8 * j + 8] for start in (24, 64, 104))
        solved = plain - from_start * before - alpha * after
        for a in range(8):
            source_ref[j : j + 1, 128 * a : 128 * a + 128] = solved[a : a + 1]


VMEM = pl.BlockSpec(memory_space=pltpu.VMEM)
SMEM = pl.BlockSpec(memory_space=pltpu.SMEM)


def call(kernel, name, outs, *operands, scalars=0, aliases=None, work_ahead=0):
    specs = [SMEM] * scalars + [VMEM] * (len(operands) - scalars)
    shapes = [jax.ShapeDtypeStruct(shape, dtype) for shape, dtype in outs]
    return pl.pallas_call(
        kernel,
        out_shape=shapes,
        in_specs=specs,
        out_specs=[VMEM] * len(outs),
        input_output_aliases=aliases or {},
        compiler_params=pltpu.CompilerParams(vmem_limit_bytes=8 * 1024 * 1024),
        cost_estimate=pl.CostEstimate(flops=work_ahead, bytes_accessed=0, transcendentals=0) if work_ahead else None,
        name=name,
    )(*operands)


def ring_parts(value, axis):
    count = lax.axis_size(axis)
    return [value] + [
        lax.ppermute(value, axis, [(at, (at + step) % count) for at in range(count)]) for step in (1, 3, 2)
    ]


def crossing(value, step):
    chips = lax.axis_size("tm_0")
    pairs = [(2 * at + core, 2 * ((at + step) % chips) + 1 - core) for at in range(chips) for core in range(2)]
    return lax.ppermute(value, TM, pairs)


def to_twin(value):
    return lax.ppermute(value, "tm_1", [(0, 1), (1, 0)])


def tm_parts(value):
    value = value + to_twin(value)
    return ring_parts(value, "tm_0")


def sky_parts(knots):
    own, one, three, two = ring_parts(knots, "sky_1")
    return ring_parts((one + three) + (two + own), "sky_0")


KNOTS = ((72, 256), f32)
GHOSTS = ((32, 128), f32)
SUMS = ((56, 128), f32)


def shards(obs_source, obs_knot, obs_count, src_design, att_design, obs_phase, obs_value, src_prior):
    at = lax.axis_index(TM)
    first = (at == 0).astype(jnp.int32).reshape(1)
    last = (at == lax.axis_size(TM) - 1).astype(jnp.int32).reshape(1)
    tm = at.astype(jnp.int32).reshape(1)
    place = lax.axis_index(SKY).astype(jnp.int32).reshape(1)
    line = lambda value: value.reshape(1, OBS_DEV)
    (state,) = call(open_kernel, "open", [STATE], work_ahead=1 << 32)
    work, sums, state = call(
        source_kernel,
        "source_sums",
        [WORK, ((160, 128), f32), STATE],
        obs_count, first, line(obs_source), src_design, line(obs_value), src_prior, state,
        aliases={6: 2},
        scalars=2,
    )
    twin_sums = to_twin(sums)
    earlier, later, twin = call(
        ghost_kernel,
        "ghosts",
        [GHOSTS] * 3,
        obs_count, tm, obs_knot.reshape(32, 128), line(obs_knot), line(obs_source), src_design, att_design, line(obs_phase), work,
        scalars=2,
    )
    sums = sums + twin_sums
    onward = jnp.concatenate([sums, later], axis=0)
    parts = (
        onward,
        crossing(onward, 1),
        crossing(jnp.concatenate([sums, earlier], axis=0), -1),
        lax.ppermute(sums, "tm_0", [(at, (at + 2) % 4) for at in range(4)]),
        to_twin(twin),
    )
    (work,) = call(
        knot_kernel,
        "knot_spread",
        [WORK],
        obs_count, last, line(obs_knot), att_design, line(obs_phase), work,
        scalars=2,
        aliases={5: 0},
    )
    knots, work, state = call(
        first_kernel, "first", [KNOTS, WORK, STATE], tm, *parts, work, state, scalars=1, aliases={6: 1, 7: 2}
    )
    parts = sky_parts(knots)
    kept = dict(scalars=1, aliases={5: 1, 6: 2})
    sums, work, state = call(start_kernel, "start", [SUMS, WORK, STATE], tm, *parts, work, state, **kept)
    parts = tm_parts(sums)
    knots, work, state = call(back_kernel, "back", [KNOTS, WORK, STATE], tm, *parts, work, state, **kept)
    parts = sky_parts(knots)
    sums, work, state = call(next_kernel, "next", [SUMS, WORK, STATE], tm, *parts, work, state, **kept)
    parts = tm_parts(sums)
    blocks, own, work, state = call(
        back_to_owners_kernel,
        "back_to_owners",
        [((16, 16, 128), f32), OWN, WORK, STATE],
        tm, place, *parts, work, state,
        scalars=2,
        aliases={6: 2, 7: 3},
    )
    blocks, own = lax.optimization_barrier((blocks, own))
    blocks = lax.all_to_all(blocks, SKY, 0, 0, tiled=True)
    return call(
        last_kernel,
        "last",
        [((4, 1, 256), f32), ((4, 1, 256), f32), ((5, 1024), f32)],
        blocks, own,
    )


def solution(mesh):
    torus = Mesh(mesh.devices.reshape(4, 4, 4, 2), SKY_TM)
    placed = (
        P(SKY_TM),
        P(SKY_TM),
        P(SKY_TM),
        P(None, SKY_TM),
        P(None, SKY_TM),
        P(SKY_TM),
        P(SKY_TM),
        P(None, SKY),
    )
    return jax.shard_map(
        shards,
        mesh=torus,
        in_specs=placed,
        out_specs=(P(None, TM, SKY), P(None, TM, SKY), P(None, SKY)),
        check_vma=False,
    )
```
